512 devices in a mesh: gx: 32 (over z, core), gy: 16 (over y, x).
Axes of the slice: x: 4, y: 4, z: 16, core: 2. Of those that a mesh axis runs over, the one named last changes fastest.
Arguments:
- residual: float32 [3, 512, 256, 128], P(None, 'gx', 'gy'), may hold values from -6 to 6
- stiffness: float32 [512, 256], P('gx', 'gy'), may hold values from 0.5 to 2
- local_inverse: bfloat16 [32, 16, 1024, 1024], P('gx', 'gy'), as said below
- coarse_basis: bfloat16 [32, 16, 8, 1024], P('gx', 'gy'), may hold values from -0.5 to 0.5
- coarse_rows: bfloat16 [32, 16, 8, 4096], P('gx', 'gy'), as said below
- send_rows: int32 [32, 16, 4, 64], P('gx', 'gy'), may hold values from 0 to 767, as said below
- partition_map: int32 [512], replicated, may hold values from 0 to 511, as said below
Outputs:
- solution: float32 [3, 512, 256, 128], P(None, 'gx', 'gy')
- final: float32 [3, 512, 256, 128], P(None, 'gx', 'gy')
The draws below stay inside these ranges and needn't reach their ends.
Inputs may be any that keep to these rules, and one draw needn't show every extreme that they name: `send_rows`: for each subdomain, the lists j = 0, 1 (lower and upper neighbour along gx) and j = 2, 3 (lower and upper neighbour along gy) each name 64 distinct owned rows, all of them in the two layers of cells nearest that neighbour. `partition_map`: A permutation of the device numbers. `coarse_rows`: with its columns put in device order through partition_map, the 4096-square matrix S is symmetric. `local_inverse`: each subdomain's block is symmetric.
All inputs are finite; a program needn't handle non-finite values.
Results may differ from the reference program's by a relative error of at most 0.0057.
Values may be sent and summed in bfloat16 or wider, within the bound.
No kernel may reach another device: no remote copies, remote signals or barrier semaphores. Data moves between devices by JAX's collectives and lax.ppermute only.
A program may use at most 64 MiB of HBM per device.

```python
import math
import jax
import jax.numpy as jnp
from jax import lax

NV = 128
CX = 16
CY = 16
OV = 64
K = 8
M = 1024
NX = 512
NY = 256
KD = 4096
N_GX = 32
N_GY = 16


def draw_local_inverse(key, part):
    device_count = NX // CX * (NY // CY)
    lower_end, upper_end, spread = (0.12, 0.26, 0.06)

    def one_block(number):
        block_key = jax.random.fold_in(key, number)
        noise_draw = jax.random.normal(jax.random.fold_in(block_key, 1), (M, M), jnp.float32)
        diagonal = jax.random.uniform(jax.random.fold_in(block_key, 2), (M,), jnp.float32, lower_end, upper_end)
        symmetric = (noise_draw + noise_draw.T) * (spread / math.sqrt(2.0 * M))
        return (symmetric + jnp.diag(diagonal)).astype(jnp.bfloat16)
    blocks = lax.map(one_block, jnp.arange(device_count, dtype=jnp.int32))
    return blocks.reshape(NX // CX, NY // CY, M, M)


def coarse_order(key):
    device_count = NX // CX * (NY // CY)
    return jax.random.permutation(jax.random.fold_in(key, 7), device_count).astype(jnp.int32)


def draw_partition_map(key, part):
    return coarse_order(key)


def draw_coarse_rows(key, part):
    device_count = NX // CX * (NY // CY)
    order_size = K * device_count
    back_scale, link_scale = (0.1, 0.25)
    noise_draw = jax.random.normal(jax.random.fold_in(key, 11), (order_size, order_size), jnp.float32)
    background = (noise_draw + noise_draw.T) * (back_scale / math.sqrt(2.0 * order_size))
    diagonal = jax.random.uniform(jax.random.fold_in(key, 12), (order_size,), jnp.float32, 0.1, 0.2)
    partners = jax.random.permutation(jax.random.fold_in(key, 13), device_count)
    first_half = partners[0::2]
    second_half = partners[1::2]
    link_blocks = jax.random.normal(jax.random.fold_in(key, 14), (device_count // 2, K, K), jnp.float32)
    link_blocks = link_blocks * (link_scale / math.sqrt(K))
    pair_terms = jnp.zeros((device_count, K, device_count, K), jnp.float32)
    pair_terms = pair_terms.at[first_half, :, second_half, :].set(link_blocks)
    pair_terms = pair_terms.at[second_half, :, first_half, :].set(jnp.swapaxes(link_blocks, 1, 2))
    whole_matrix = background + pair_terms.reshape(order_size, order_size) + jnp.diag(diagonal)
    positions = coarse_order(key)
    stored = jnp.zeros((order_size, device_count, K), jnp.float32)
    stored = stored.at[:, positions, :].set(whole_matrix.reshape(order_size, device_count, K))
    return stored.astype(jnp.bfloat16).reshape(NX // CX, NY // CY, K, order_size)


def draw_send_rows(key, part):
    device_count = NX // CX * (NY // CY)
    key_list = jax.random.split(key, device_count * 4)
    across_picks = jax.vmap(lambda one_key: jax.random.permutation(one_key, 6 * CY)[:OV])(key_list[:2 * device_count])
    along_picks = jax.vmap(lambda one_key: jax.random.permutation(one_key, 6 * CX)[:OV])(key_list[2 * device_count:])
    across_picks = across_picks.reshape(device_count, 2, OV)
    along_picks = along_picks.reshape(device_count, 2, OV)
    side_index = jnp.arange(2, dtype=jnp.int32)[None, :, None]
    component = across_picks // (2 * CY)
    remainder = across_picks % (2 * CY)
    layer_index = remainder // CY
    first_cell = jnp.where(side_index == 0, layer_index, CX - 1 - layer_index)
    across_rows = component * CX * CY + first_cell * CY + remainder % CY
    component = along_picks // (2 * CX)
    remainder = along_picks % (2 * CX)
    layer_index = remainder // CX
    second_cell = jnp.where(side_index == 0, layer_index, CY - 1 - layer_index)
    along_rows = component * CX * CY + remainder % CX * CY + second_cell
    all_rows = jnp.concatenate([across_rows, along_rows], axis=1)
    return all_rows.reshape(NX // CX, NY // CY, 4, OV).astype(jnp.int32)


def shard_levels(key, extent, cuts, smallest, high):
    level, own = 1.0, jax.random.fold_in(key, 6)
    for axis_at, blocks in cuts:
        heights = jnp.exp(jax.random.uniform(jax.random.fold_in(own, axis_at), (blocks,), jnp.float32, smallest / len(cuts), high / len(cuts)))
        level = level * jnp.repeat(heights, extent[axis_at] // blocks).reshape([-1 if axis == axis_at else 1 for axis in range(len(extent))])
    return level


def gaussian(own_key, extent, scale, bound, shards=(), kind=jnp.bfloat16):
    values = jax.random.normal(own_key, extent, jnp.float32) * scale
    if len(shards) > 0:
        values = shard_levels(own_key, extent, shards, -0.22, 0.18) * values
    return jnp.clip(values, min=-bound, max=bound).astype(kind)


def setup_inputs(seed: int = 0) -> dict:
    key_of = jax.random.split(jax.random.key(seed), 8)
    return {
        "residual": gaussian(key_of[0], (3, NX, NY, NV), 1.0, 6.0, ((1, 32), (2, 16)), jnp.float32),
        "stiffness": jnp.clip(jnp.exp(math.log(2.0) - 1.3862944 * jax.random.uniform(key_of[1], (NX, NY), jnp.float32) ** shard_levels(key_of[1], (NX, NY), ((0, 32), (1, 16)), -0.2, 0.2)), 0.5, 2.0),
        "local_inverse": draw_local_inverse(jax.random.fold_in(key_of[7], 71), 0),
        "coarse_basis": gaussian(key_of[3], (N_GX, N_GY, K, M), 0.08, 0.5, ((0, 32), (1, 16))),
        "coarse_rows": draw_coarse_rows(jax.random.fold_in(key_of[7], 71), 0),
        "send_rows": draw_send_rows(jax.random.fold_in(key_of[7], 71), 0),
        "partition_map": draw_partition_map(jax.random.fold_in(key_of[7], 71), 0),
    }


def from_lower(blocks, axis):
    edge = jnp.zeros_like(lax.slice_in_dim(blocks, 0, 1, axis=axis))
    return jnp.concatenate([edge, lax.slice_in_dim(blocks, 0, blocks.shape[axis] - 1, axis=axis)], axis=axis)


def from_upper(blocks, axis):
    edge = jnp.zeros_like(lax.slice_in_dim(blocks, 0, 1, axis=axis))
    return jnp.concatenate([lax.slice_in_dim(blocks, 1, blocks.shape[axis], axis=axis), edge], axis=axis)


def pick_rows(matrix, picks):
    return jnp.take(matrix, picks, axis=0)


def project_down(group):
    return jnp.dot(group[0], group[1], preferred_element_type=jnp.float32)


def apply_local(group):
    local_part = jnp.dot(group[0], group[1], preferred_element_type=jnp.float32)
    return local_part + jnp.dot(group[2].T, group[3], preferred_element_type=jnp.float32)


def add_back(update, picks, incoming):
    update = update.at[picks[0]].add(incoming[0])
    update = update.at[picks[1]].add(incoming[1])
    update = update.at[picks[2]].add(incoming[2])
    return update.at[picks[3]].add(incoming[3])


def operate(values, stiffness):
    padded = jnp.pad(values, ((0, 0), (1, 1), (1, 1), (0, 0)))
    beside = padded[:, 2:, 1:-1] + padded[:, :-2, 1:-1] + padded[:, 1:-1, 2:] + padded[:, 1:-1, :-2]
    return (4.0 + stiffness[None, :, :, None]) * values - beside


def correct(values, local_inverse, coarse_basis, coarse_rows, send_rows, partition_map):
    grid_rows = N_GX
    grid_cols = N_GY
    device_count = grid_rows * grid_cols
    own_count = 3 * CX * CY
    own_rows = values.reshape(3, grid_rows, CX, grid_cols, CY, NV).transpose(1, 3, 0, 2, 4, 5)
    own_rows = own_rows.reshape(grid_rows, grid_cols, own_count, NV)
    outgoing = jax.vmap(jax.vmap(pick_rows))(own_rows, send_rows)
    subdomain = jnp.concatenate([own_rows, from_lower(outgoing[:, :, 1], 0), from_upper(outgoing[:, :, 0], 0),
                                 from_lower(outgoing[:, :, 3], 1), from_upper(outgoing[:, :, 2], 1)], axis=2)
    subdomain = subdomain.astype(jnp.bfloat16)
    flat_sub = subdomain.reshape(device_count, M, NV)
    flat_inverse = local_inverse.reshape(device_count, M, M)
    flat_basis = coarse_basis.reshape(device_count, K, M)
    coarse_in = lax.map(project_down, (flat_basis, flat_sub)).astype(jnp.bfloat16)
    whole_matrix = coarse_rows.reshape(KD, device_count, K)[:, partition_map, :].reshape(KD, KD)
    coarse_out = jnp.dot(whole_matrix, coarse_in.reshape(KD, NV), preferred_element_type=jnp.float32)
    coarse_out = coarse_out.astype(jnp.bfloat16).reshape(device_count, K, NV)
    patch = lax.map(apply_local, (flat_inverse, flat_sub, flat_basis, coarse_out)).reshape(grid_rows, grid_cols, M, NV)
    own_patch = patch[:, :, :own_count]
    back_zero = from_lower(patch[:, :, own_count + OV:own_count + 2 * OV], 0)
    back_one = from_upper(patch[:, :, own_count:own_count + OV], 0)
    back_two = from_lower(patch[:, :, own_count + 3 * OV:], 1)
    back_three = from_upper(patch[:, :, own_count + 2 * OV:own_count + 3 * OV], 1)
    incoming = jnp.stack([back_zero, back_one, back_two, back_three], axis=2)
    update = jax.vmap(jax.vmap(add_back))(own_patch, send_rows, incoming)
    update = update.reshape(grid_rows, grid_cols, 3, CX, CY, NV).transpose(2, 0, 3, 1, 4, 5)
    return update.reshape(3, NX, NY, NV)


def reference(residual, stiffness, local_inverse, coarse_basis, coarse_rows, send_rows, partition_map):
    first_pass = correct(residual, local_inverse, coarse_basis, coarse_rows, send_rows, partition_map)
    middle = residual - operate(first_pass, stiffness)
    second_pass = correct(middle, local_inverse, coarse_basis, coarse_rows, send_rows, partition_map)
    solution = first_pass + second_pass
    return solution, residual - operate(solution, stiffness)
```

```python
import jax
import jax.numpy as jnp
from jax import lax
from jax.sharding import PartitionSpec as P


def with_halo(block, sides, width):
    for axis, dim in sides:
        count = lax.axis_size(axis)
        forward = [(i, i + 1) for i in range(count - 1)]
        backward = [(target, source) for source, target in forward]
        low = lax.ppermute(
            lax.slice_in_dim(block, block.shape[dim] - width, None, axis=dim), axis, forward
        )
        high = lax.ppermute(lax.slice_in_dim(block, 0, width, axis=dim), axis, backward)
        block = jnp.concatenate([low, block, high], axis=dim)
    return block


def trade_along_gx(pair):
    return with_halo(pair, (("gx", 0),), 1)


def trade_along_gy(pair):
    return with_halo(pair, (("gy", 0),), 1)


def operate(values, stiffness):
    padded = with_halo(values, (("gx", 1), ("gy", 2)), 1)
    beside = padded[:, 2:, 1:-1] + padded[:, :-2, 1:-1] + padded[:, 1:-1, 2:] + padded[:, 1:-1, :-2]
    return (4.0 + stiffness[None, :, :, None]) * values - beside


def coarse_solve(coarse_in, crossing):
    count = lax.axis_size("gx")
    copies = jnp.broadcast_to(coarse_in[None], (count,) + coarse_in.shape)
    column = lax.all_to_all(copies, "gx", split_axis=0, concat_axis=0, tiled=True)
    parts = jnp.dot(
        crossing, column.reshape(-1, coarse_in.shape[-1]), preferred_element_type=jnp.float32
    )
    parts = parts.reshape(lax.axis_size("gy"), *coarse_in.shape)
    return jnp.sum(lax.all_to_all(parts, "gy", split_axis=0, concat_axis=0, tiled=True), axis=0)


def precondition(values, inverse, basis_rows, row_lists, ordered):
    own_rows = values.reshape(-1, values.shape[-1])
    own_count = own_rows.shape[0]
    margin = row_lists.shape[1]
    outgoing = jnp.take(own_rows, row_lists, axis=0)
    from_gx = trade_along_gx(outgoing[0:2])
    from_gy = trade_along_gy(outgoing[2:4])
    subdomain = jnp.concatenate([own_rows, from_gx[0], from_gx[3], from_gy[0], from_gy[3]], axis=0)
    subdomain = subdomain.astype(jnp.bfloat16)
    coarse_in = jnp.dot(basis_rows, subdomain, preferred_element_type=jnp.float32).astype(
        jnp.bfloat16
    )
    coarse_out = coarse_solve(coarse_in, ordered).astype(jnp.bfloat16)
    patch = jnp.dot(inverse, subdomain, preferred_element_type=jnp.float32)
    patch = patch + lax.dot_general(
        basis_rows, coarse_out, (((0,), (0,)), ((), ())), preferred_element_type=jnp.float32
    )
    back_gx = trade_along_gx(
        jnp.stack(
            [
                patch[own_count : own_count + margin],
                patch[own_count + margin : own_count + 2 * margin],
            ]
        )
    )
    back_gy = trade_along_gy(
        jnp.stack(
            [
                patch[own_count + 2 * margin : own_count + 3 * margin],
                patch[own_count + 3 * margin :],
            ]
        )
    )
    update = patch[:own_count]
    update = update.at[row_lists[0]].add(back_gx[0])
    update = update.at[row_lists[1]].add(back_gx[3])
    update = update.at[row_lists[2]].add(back_gy[0])
    update = update.at[row_lists[3]].add(back_gy[3])
    return update.reshape(values.shape)


def per_device(
    residual, stiffness, local_inverse, coarse_basis, coarse_rows, send_rows, partition_map
):
    inverse = local_inverse[0, 0]
    basis_rows = coarse_basis[0, 0]
    row_lists = send_rows[0, 0]
    device_count = partition_map.shape[0]
    coarse_width = basis_rows.shape[0]
    stored = coarse_rows[0, 0].reshape(coarse_width, device_count, coarse_width)
    chosen = (partition_map[None, :] == jnp.arange(device_count)[:, None]).astype(stored.dtype)
    ordered = jnp.einsum("ipk,pe->iek", stored, chosen)
    grid = (coarse_width, lax.axis_size("gx"), lax.axis_size("gy"), coarse_width)
    ordered = ordered.reshape(grid).transpose(2, 0, 1, 3).reshape(grid[2], coarse_width, -1)
    ordered = lax.all_to_all(ordered, "gy", split_axis=0, concat_axis=0, tiled=True)
    ordered = ordered.reshape(grid[2] * coarse_width, -1)
    first_pass = precondition(residual, inverse, basis_rows, row_lists, ordered)
    middle = residual - operate(first_pass, stiffness)
    second_pass = precondition(middle, inverse, basis_rows, row_lists, ordered)
    solution = first_pass + second_pass
    return (solution, residual - operate(solution, stiffness))


def solution(mesh):
    placed = (
        P(None, "gx", "gy", None),
        P("gx", "gy"),
        P("gx", "gy", None, None),
        P("gx", "gy", None, None),
        P("gx", "gy", None, None),
        P("gx", "gy", None, None),
        P(),
    )
    return jax.shard_map(
        per_device,
        mesh=mesh,
        in_specs=placed,
        out_specs=(P(None, "gx", "gy", None), P(None, "gx", "gy", None)),
        check_vma=False,
    )
```

```python
import functools

import jax
import jax.numpy as jnp
from jax import lax
from jax.experimental import pallas as pl
from jax.experimental.pallas import tpu as pltpu
from jax.sharding import PartitionSpec as P

F32, BF16 = jnp.float32, jnp.bfloat16
COMPONENTS, CELLS, LANES = 3, 16, 128
OWN = COMPONENTS * CELLS * CELLS
MARGIN = 64
SIDE, ABOVE = 24, 4
PLANE = SIDE * SIDE
FIELD = COMPONENTS * PLANE
BESIDE = COMPONENTS * CELLS * 8
STRIP = COMPONENTS * 2 * CELLS
EDGE = STRIP + 2 * CELLS + 8
PART = 128
TRADE = COMPONENTS * PART


def at(component, row, column=0):
    return component * PLANE + (row + ABOVE) * SIDE + column % SIDE


def column_of(component, column, first=0, count=CELLS):
    return pl.ds(at(component, first, column), count, stride=SIDE)


def matmul(a, b, contract=(1, 0)):
    return lax.dot_general(
        a, b, (((contract[0],), (contract[1],)), ((), ())), preferred_element_type=F32
    )


def call(kernel, outs, *args, scratch=(), smem=(), aliases=None):
    vmem, scalar = pl.BlockSpec(memory_space=pltpu.VMEM), pl.BlockSpec(memory_space=pltpu.SMEM)
    return pl.pallas_call(
        kernel,
        out_shape=[jax.ShapeDtypeStruct(shape, kind) for shape, kind in outs],
        in_specs=[scalar if i in smem else vmem for i in range(len(args))],
        out_specs=[vmem] * len(outs),
        scratch_shapes=[pltpu.VMEM(shape, kind) for shape, kind in scratch],
        input_output_aliases=aliases or {},
        compiler_params=pltpu.CompilerParams(vmem_limit_bytes=24 * 2**20),
    )(*args)


def order_rows(rows_ref, places_ref, out_ref, tiles):
    n_tiles, n_gy, n_groups = tiles.shape[0], out_ref.shape[0], out_ref.shape[2] // LANES
    for t in range(n_tiles):
        tiles[t] = rows_ref[:, t * LANES : (t + 1) * LANES].astype(F32)
    slot = lax.broadcasted_iota(jnp.int32, (8, LANES), 1) // 8

    def one(b, carry):
        for group in range(n_groups):
            block = jnp.zeros((8, LANES), F32)
            for q in range(16):
                place = places_ref[(group * 16 + q) * n_gy + b]
                tile = tiles[lax.shift_right_logical(place, 4)]
                turned = pltpu.roll(tile, ((q + 16 - (place & 15)) & 15) * 8, 1)
                block = jnp.where(slot == q, turned, block)
            out_ref[b, :, group * LANES : (group + 1) * LANES] = block
        return carry

    lax.fori_loop(0, n_gy, one, 0)


def make_edges(values_ref, stiff_ref, turned_ref, lists_ref, up_ref, down_ref, left_ref, right_ref):
    lists = lists_ref[...]
    component, i, j = lists >> 8, (lists >> 4) & 15, lists & 15
    codes = (
        component * 32 + i * 16 + j,
        component * 32 + (i - 14) * 16 + j,
        component * 128 + i * 8 + j,
        component * 128 + i * 8 + j - 8,
    )
    for side, ref in enumerate((up_ref, down_ref, left_ref, right_ref)):
        first = 0 if side in (0, 2) else CELLS - 2
        for c in range(COMPONENTS):
            for layer in range(2):
                if side < 2:
                    rows = pl.ds(c * 256 + (first + layer) * CELLS, CELLS)
                else:
                    rows = pl.ds(c * 256 + first + layer, CELLS, stride=CELLS)
                ref[pl.ds((c * 2 + layer) * CELLS, CELLS), :] = values_ref[rows, :]
        for layer in range(2):
            source = turned_ref if side < 2 else stiff_ref
            one = source[:, first + layer : first + layer + 1]
            ref[pl.ds(STRIP + layer * CELLS, CELLS), :] = jnp.broadcast_to(one, (CELLS, LANES))
        code = (codes[side][side : side + 1] + 1).astype(F32)
        ref[pl.ds(STRIP + 2 * CELLS, 8), 0:MARGIN] = jnp.broadcast_to(code, (8, MARGIN))


def restrict(own, strips, beside, across_ref, along_ref, basis_ref, sub_ref, coarse_ref):
    sub_ref[OWN : OWN + 2 * MARGIN] = matmul(across_ref[...], strips.astype(BF16), (0, 0)).astype(BF16)
    sub_ref[OWN + 2 * MARGIN :] = matmul(along_ref[...], beside.astype(BF16), (0, 0)).astype(BF16)
    coarse = matmul(basis_ref[...], sub_ref[...]).astype(BF16).astype(F32)
    for a in range(coarse_ref.shape[0]):
        coarse_ref[a] = coarse


def start_pass(
    values_ref, up_ref, down_ref, left_ref, right_ref, stiff_ref, turned_ref, basis_ref,
    field_ref, diagonal_ref, across_ref, along_ref, sub_ref, coarse_ref,
):
    field_ref[...] = jnp.zeros_like(field_ref)
    diagonal_ref[...] = jnp.full(diagonal_ref.shape, 4.0, F32)
    for c in range(COMPONENTS):
        for i in range(CELLS):
            rows = values_ref[c * 256 + i * CELLS : c * 256 + (i + 1) * CELLS]
            field_ref[pl.ds(at(c, i), CELLS), :] = rows
            sub_ref[c * 256 + i * CELLS : c * 256 + (i + 1) * CELLS] = rows.astype(BF16)
        for layer in range(2):
            rows = pl.ds((c * 2 + layer) * CELLS, CELLS)
            field_ref[pl.ds(at(c, layer - 2), CELLS), :] = up_ref[rows, :]
            field_ref[pl.ds(at(c, layer + CELLS), CELLS), :] = down_ref[rows, :]
            field_ref[column_of(c, layer - 2), :] = left_ref[rows, :]
            field_ref[column_of(c, layer + CELLS), :] = right_ref[rows, :]
    for i in range(CELLS):
        diagonal_ref[pl.ds(at(0, i), CELLS), :] += jnp.broadcast_to(turned_ref[:, i : i + 1], (CELLS, LANES))
    for layer in range(2):
        rows = pl.ds(STRIP + layer * CELLS, CELLS)
        diagonal_ref[pl.ds(at(0, layer - 2), CELLS), :] += up_ref[rows, :]
        diagonal_ref[pl.ds(at(0, layer + CELLS), CELLS), :] += down_ref[rows, :]
        diagonal_ref[column_of(0, layer - 2), :] += left_ref[rows, :]
        diagonal_ref[column_of(0, layer + CELLS), :] += right_ref[rows, :]

    def chosen(ref, rows):
        code = ref[STRIP + 2 * CELLS : STRIP + 2 * CELLS + 1, 0:MARGIN]
        spot = lax.broadcasted_iota(jnp.int32, (rows, MARGIN), 0).astype(F32) + 1.0
        return jnp.where(spot == code, 1.0, 0.0)

    none = jnp.zeros((STRIP, MARGIN), F32)
    across_ref[...] = jnp.concatenate(
        [
            jnp.concatenate([chosen(up_ref, STRIP), none], axis=1),
            jnp.concatenate([none, chosen(down_ref, STRIP)], axis=1),
        ],
        axis=0,
    ).astype(BF16)
    along_ref[...] = jnp.concatenate(
        [chosen(left_ref, BESIDE), chosen(right_ref, BESIDE)], axis=1
    ).astype(BF16)
    strips = jnp.concatenate([up_ref[0:STRIP], down_ref[0:STRIP]], axis=0)
    beside = jnp.concatenate(
        [field_ref[pl.ds(at(c, i, CELLS), 8), :] for c in range(COMPONENTS) for i in range(CELLS)], axis=0
    )
    restrict(None, strips, beside, across_ref, along_ref, basis_ref, sub_ref, coarse_ref)


def cross_multiply(rows_ref, column_ref, parts_ref):
    n_gy, k, width = rows_ref.shape
    rows = rows_ref[...].reshape(n_gy * k, width).astype(BF16)
    parts_ref[...] = matmul(rows, column_ref[...].reshape(width, LANES).astype(BF16)).reshape(parts_ref.shape)


def apply_patch(sub_ref, inverse_ref, basis_ref, parts_ref, across_ref, along_ref, field_ref, up_ref, down_ref, patch):
    coarse = jnp.sum(parts_ref[...], axis=0).astype(BF16)
    patch[...] = matmul(inverse_ref[...], sub_ref[...]) + matmul(basis_ref[...], coarse, (0, 0))
    field_ref[...] = jnp.zeros_like(field_ref)
    across = matmul(across_ref[...], patch[OWN : OWN + 2 * MARGIN].astype(BF16))
    along = matmul(along_ref[...], patch[OWN + 2 * MARGIN :].astype(BF16))
    for c in range(COMPONENTS):
        for i in range(CELLS):
            n = c * CELLS + i
            field_ref[pl.ds(at(c, i), CELLS), :] = patch[n * CELLS : (n + 1) * CELLS]
            field_ref[pl.ds(at(c, i, CELLS), 8), :] = along[n * 8 : (n + 1) * 8]
        for layer in range(2):
            n = (c * 2 + layer) * CELLS
            field_ref[pl.ds(at(c, layer - 2), CELLS), :] = across[n : n + CELLS]
            field_ref[pl.ds(at(c, layer + CELLS), CELLS), :] = across[STRIP + n : STRIP + n + CELLS]
        up_ref[c * PART : (c + 1) * PART] = field_ref[pl.ds(at(c, -2), PART), :].astype(BF16)
        down_ref[c * PART : (c + 1) * PART] = field_ref[pl.ds(at(c, CELLS - 3), PART), :].astype(BF16)


def add_across(field_ref, up_ref, down_ref, out_ref, left_ref, right_ref, strip):
    out_ref[...] = field_ref[...]
    for c in range(COMPONENTS):
        part = slice(c * PART, (c + 1) * PART)
        out_ref[pl.ds(at(c, -3), 5 * SIDE), :] += up_ref[part].astype(F32)[: 5 * SIDE]
        out_ref[pl.ds(at(c, CELLS - 2), 5 * SIDE), :] += down_ref[part].astype(F32)[: 5 * SIDE]
    for first, ref in ((-2, left_ref), (CELLS - 3, right_ref)):
        for c in range(COMPONENTS):
            for q in range(5):
                strip[pl.ds(q * SIDE, SIDE), :] = out_ref[column_of(c, first + q, -ABOVE, SIDE), :]
            strip[5 * SIDE :] = jnp.zeros((PART - 5 * SIDE, LANES), F32)
            ref[c * PART : (c + 1) * PART] = strip[...].astype(BF16)


def add_along(field_ref, left_ref, right_ref):
    for c in range(COMPONENTS):
        for first, ref in ((-3, left_ref), (CELLS - 2, right_ref)):
            came = ref[c * PART : (c + 1) * PART].astype(F32)
            for q in range(5):
                where = column_of(c, first + q, -ABOVE, SIDE)
                field_ref[where, :] = field_ref[where, :] + came[q * SIDE : (q + 1) * SIDE]


def operate_row(field, diagonal_ref, c, i):
    here = field(c, i)
    beside = field(c, i - 1) + field(c, i + 1) + pltpu.roll(here, 1, 0) + pltpu.roll(here, SIDE - 1, 0)
    return diagonal_ref[pl.ds(at(0, i), SIDE), :] * here - beside


def middle_pass(
    field_ref, left_ref, right_ref, values_ref, diagonal_ref, across_ref, along_ref, basis_ref,
    first_ref, sub_ref, coarse_ref, strips, beside,
):
    first_ref[...] = field_ref[...]
    add_along(first_ref, left_ref, right_ref)

    def field(c, i):
        return first_ref[pl.ds(at(c, i), SIDE), :]

    for c in range(COMPONENTS):
        for i in range(-2, CELLS + 2):
            middle = values_ref[pl.ds(at(c, i), SIDE), :] - operate_row(field, diagonal_ref, c, i)
            if 0 <= i < CELLS:
                n = c * CELLS + i
                sub_ref[n * CELLS : (n + 1) * CELLS] = middle[:CELLS].astype(BF16)
                beside[pl.ds(n * 8, 8), :] = middle[CELLS:]
            else:
                n = (c * 2 + (i + 2 if i < 0 else i - CELLS)) * CELLS + (0 if i < 0 else STRIP)
                strips[pl.ds(n, CELLS), :] = middle[:CELLS]
    restrict(None, strips[...], beside[...], across_ref, along_ref, basis_ref, sub_ref, coarse_ref)


def last_pass(field_ref, left_ref, right_ref, first_ref, values_ref, diagonal_ref, solution_ref, final_ref, total):
    total[...] = field_ref[...]
    add_along(total, left_ref, right_ref)
    total[...] += first_ref[...]

    def field(c, i):
        return total[pl.ds(at(c, i), SIDE), :]

    for c in range(COMPONENTS):
        for i in range(CELLS):
            rows = slice((c * CELLS + i) * CELLS, (c * CELLS + i + 1) * CELLS)
            solution_ref[rows] = total[pl.ds(at(c, i), CELLS), :]
            applied = operate_row(field, diagonal_ref, c, i)[:CELLS]
            final_ref[rows] = values_ref[pl.ds(at(c, i), CELLS), :] - applied


def trade(lower, upper, axis):
    count = lax.axis_size(axis)
    forward = [(i, i + 1) for i in range(count - 1)]
    backward = [(target, source) for source, target in forward]
    return lax.ppermute(upper, axis, forward), lax.ppermute(lower, axis, backward)


def per_device(residual, stiffness, local_inverse, coarse_basis, coarse_rows, send_rows, partition_map):
    inverse, basis, lists = local_inverse[0, 0], coarse_basis[0, 0], send_rows[0, 0]
    k, order = coarse_rows.shape[2:]
    n_gx, n_gy = lax.axis_size("gx"), lax.axis_size("gy")
    values = residual.reshape(OWN, LANES)
    turned = stiffness.T
    swap = functools.partial(lax.all_to_all, split_axis=0, concat_axis=0, tiled=True)

    edge = ((EDGE, LANES), F32)
    up, down, left, right = call(make_edges, [edge] * 4, values, stiffness, turned, lists)
    [crossing] = call(
        order_rows, [((n_gy, k, n_gx * k), F32)], coarse_rows[0, 0], partition_map,
        scratch=[((order // LANES, k, LANES), F32)], smem=(1,),
    )
    crossing = swap(crossing, "gy")
    up, down = trade(up, down, "gx")
    left, right = trade(left, right, "gy")

    field = ((FIELD, LANES), F32)
    copies = ((n_gx, k, LANES), F32)
    sub_kind = ((OWN + 4 * MARGIN, LANES), BF16)
    part = ((TRADE, LANES), BF16)
    ambient, diagonal, across, along, sub, coarse = call(
        start_pass,
        [field, ((PLANE, LANES), F32), ((2 * STRIP, 2 * MARGIN), BF16), ((BESIDE, 2 * MARGIN), BF16), sub_kind, copies],
        values, up, down, left, right, stiffness, turned, basis,
    )

    def correct(sub, coarse):
        [parts] = call(cross_multiply, [((n_gy, k, LANES), F32)], crossing, swap(coarse, "gx"))
        y, to_up, to_down = call(
            apply_patch, [field, part, part], sub, inverse, basis, swap(parts, "gy"), across, along,
            scratch=[((OWN + 4 * MARGIN, LANES), F32)],
        )
        y, to_left, to_right = call(
            add_across, [field, part, part], y, *trade(to_up, to_down, "gx"),
            scratch=[((PART, LANES), F32)],
        )
        return (y, *trade(to_left, to_right, "gy"))

    first, sub, coarse = call(
        middle_pass, [field, sub_kind, copies], *correct(sub, coarse), ambient, diagonal, across, along, basis,
        scratch=[((2 * STRIP, LANES), F32), ((BESIDE, LANES), F32)],
    )
    own = ((OWN, LANES), F32)
    total, final = call(
        last_pass, [own, own], *correct(sub, coarse), first, ambient, diagonal, scratch=[field]
    )
    return total.reshape(residual.shape), final.reshape(residual.shape)


def solution(mesh):
    placed = (
        P(None, "gx", "gy", None),
        P("gx", "gy"),
        P("gx", "gy", None, None),
        P("gx", "gy", None, None),
        P("gx", "gy", None, None),
        P("gx", "gy", None, None),
        P(),
    )
    return jax.shard_map(
        per_device,
        mesh=mesh,
        in_specs=placed,
        out_specs=(P(None, "gx", "gy", None), P(None, "gx", "gy", None)),
        check_vma=False,
    )
```

```python
import functools

import jax
import jax.numpy as jnp
from jax import lax
from jax.experimental import pallas as pl
from jax.experimental.pallas import tpu as pltpu
from jax.sharding import Mesh
from jax.sharding import PartitionSpec as P

F32, BF16 = jnp.float32, jnp.bfloat16
COMPONENTS, CELLS, LANES = 3, 16, 128
OWN = COMPONENTS * CELLS * CELLS
MARGIN = 64
SIDE, ABOVE = 24, 4
PLANE = SIDE * SIDE
FIELD = COMPONENTS * PLANE
BESIDE = COMPONENTS * CELLS * 8
STRIP = COMPONENTS * 2 * CELLS
EDGE = STRIP + 2 * CELLS + 8
VMEM_BYTES = 8 * 2**20


def part_of(depth):
    return -(-(depth + 2) * SIDE // 16) * 16


def at(component, row, column=0):
    return component * PLANE + (row + ABOVE) * SIDE + column % SIDE


def column_of(component, column, first=0, count=CELLS):
    return pl.ds(at(component, first, column), count, stride=SIDE)


def matmul(a, b, contract=(1, 0)):
    return lax.dot_general(
        a, b, (((contract[0],), (contract[1],)), ((), ())), preferred_element_type=F32
    )


def call(kernel, outs, *args, scratch=(), fetched=0, copies=None, cost=None):
    vmem, hbm = pl.BlockSpec(memory_space=pltpu.VMEM), pl.BlockSpec(memory_space=pltpu.HBM)
    copies = [pltpu.SemaphoreType.DMA((copies or fetched,))] if fetched else []
    return pl.pallas_call(
        kernel,
        out_shape=[jax.ShapeDtypeStruct(shape, kind) for shape, kind in outs],
        in_specs=[hbm if i < fetched else vmem for i in range(len(args))],
        out_specs=[vmem] * len(outs),
        scratch_shapes=[*(pltpu.VMEM(*s) if isinstance(s, tuple) else s for s in scratch), *copies],
        compiler_params=pltpu.CompilerParams(vmem_limit_bytes=VMEM_BYTES),
        cost_estimate=pl.CostEstimate(flops=cost[0], bytes_accessed=cost[1], transcendentals=0) if cost else None,
    )(*(pltpu.with_memory_space_constraint(a, pltpu.HBM) if i < fetched else a for i, a in enumerate(args)))


def fetch(pairs, sems):
    copies = [pltpu.make_async_copy(source, target, sems.at[i]) for i, (source, target) in enumerate(pairs)]
    for copy in copies:
        copy.start()
    for copy in copies:
        copy.wait()


def order_rows(rows_hbm, places_hbm, after_ref, out_ref, rows, places, tiles, sems):
    fetch([(rows_hbm, rows), (places_hbm, places)], sems)
    n_targets, width = out_ref.shape[0], out_ref.shape[2]
    for t in range(tiles.shape[0]):
        tiles[t] = rows[:, t * LANES : (t + 1) * LANES].astype(F32)
    slot = lax.broadcasted_iota(jnp.int32, (8, LANES), 1) // 8

    def one(target, carry):
        block = jnp.zeros((8, LANES), F32)
        for q in range(width // 8):
            place = places[q * n_targets + target]
            tile = tiles[lax.shift_right_logical(place, 4)]
            turned = pltpu.roll(tile, ((q + 16 - (place & 15)) & 15) * 8, 1)
            block = jnp.where(slot == q, turned, block)
        out_ref[target] = block[:, :width]
        return carry

    lax.fori_loop(0, n_targets, one, 0, unroll=8)


def make_edges(
    values_hbm, stiff_hbm, lists_hbm, up_ref, down_ref, left_ref, right_ref, values_ref, stiff_ref, lists_ref, sems
):
    fetch([(values_hbm, values_ref), (stiff_hbm, stiff_ref), (lists_hbm, lists_ref)], sems)
    lists = lists_ref[...]
    stiff = stiff_ref[...]
    turned = stiff.T
    component, i, j = lists >> 8, (lists >> 4) & 15, lists & 15
    codes = (
        component * 32 + i * 16 + j,
        component * 32 + (i - 14) * 16 + j,
        component * 128 + i * 8 + j,
        component * 128 + i * 8 + j - 8,
    )
    for side, ref in enumerate((up_ref, down_ref, left_ref, right_ref)):
        first = 0 if side in (0, 2) else CELLS - 2
        for c in range(COMPONENTS):
            for layer in range(2):
                if side < 2:
                    rows = pl.ds(c * 256 + (first + layer) * CELLS, CELLS)
                else:
                    rows = pl.ds(c * 256 + first + layer, CELLS, stride=CELLS)
                ref[pl.ds((c * 2 + layer) * CELLS, CELLS), :] = values_ref[rows, :]
        for layer in range(2):
            source = turned if side < 2 else stiff
            one = source[:, first + layer : first + layer + 1]
            ref[pl.ds(STRIP + layer * CELLS, CELLS), :] = jnp.broadcast_to(one, (CELLS, LANES))
        code = (codes[side][side : side + 1] + 1).astype(F32)
        ref[pl.ds(STRIP + 2 * CELLS, 8), 0:MARGIN] = jnp.broadcast_to(code, (8, MARGIN))


def restrict(strips, beside, across_ref, along_ref, basis_ref, sub_ref, coarse_ref):
    sub_ref[OWN : OWN + 2 * MARGIN] = matmul(across_ref[...], strips.astype(BF16), (0, 0)).astype(BF16)
    sub_ref[OWN + 2 * MARGIN :] = matmul(along_ref[...], beside.astype(BF16), (0, 0)).astype(BF16)
    coarse = matmul(basis_ref[...], sub_ref[...]).astype(BF16).astype(F32)
    for a in range(coarse_ref.shape[0]):
        coarse_ref[a] = coarse


def start_pass(
    values_hbm, stiff_hbm, basis_hbm, up_ref, down_ref, left_ref, right_ref,
    field_ref, diagonal_ref, across_ref, along_ref, sub_ref, basis_ref, coarse_ref,
    values_ref, stiff_ref, sems,
):
    fetch([(values_hbm, values_ref), (stiff_hbm, stiff_ref), (basis_hbm, basis_ref)], sems)
    turned = stiff_ref[...].T
    field_ref[...] = jnp.zeros_like(field_ref)
    diagonal_ref[...] = jnp.full(diagonal_ref.shape, 4.0, F32)
    for c in range(COMPONENTS):
        for i in range(CELLS):
            rows = values_ref[c * 256 + i * CELLS : c * 256 + (i + 1) * CELLS]
            field_ref[pl.ds(at(c, i), CELLS), :] = rows
            sub_ref[c * 256 + i * CELLS : c * 256 + (i + 1) * CELLS] = rows.astype(BF16)
        for layer in range(2):
            rows = pl.ds((c * 2 + layer) * CELLS, CELLS)
            field_ref[pl.ds(at(c, layer - 2), CELLS), :] = up_ref[rows, :]
            field_ref[pl.ds(at(c, layer + CELLS), CELLS), :] = down_ref[rows, :]
            field_ref[column_of(c, layer - 2), :] = left_ref[rows, :]
            field_ref[column_of(c, layer + CELLS), :] = right_ref[rows, :]
    for i in range(CELLS):
        diagonal_ref[pl.ds(at(0, i), CELLS), :] += jnp.broadcast_to(turned[:, i : i + 1], (CELLS, LANES))
    for layer in range(2):
        rows = pl.ds(STRIP + layer * CELLS, CELLS)
        diagonal_ref[pl.ds(at(0, layer - 2), CELLS), :] += up_ref[rows, :]
        diagonal_ref[pl.ds(at(0, layer + CELLS), CELLS), :] += down_ref[rows, :]
        diagonal_ref[column_of(0, layer - 2), :] += left_ref[rows, :]
        diagonal_ref[column_of(0, layer + CELLS), :] += right_ref[rows, :]

    def chosen(ref, rows):
        code = ref[STRIP + 2 * CELLS : STRIP + 2 * CELLS + 1, 0:MARGIN]
        spot = lax.broadcasted_iota(jnp.int32, (rows, MARGIN), 0).astype(F32) + 1.0
        return jnp.where(spot == code, 1.0, 0.0)

    none = jnp.zeros((STRIP, MARGIN), F32)
    across_ref[...] = jnp.concatenate(
        [
            jnp.concatenate([chosen(up_ref, STRIP), none], axis=1),
            jnp.concatenate([none, chosen(down_ref, STRIP)], axis=1),
        ],
        axis=0,
    ).astype(BF16)
    along_ref[...] = jnp.concatenate(
        [chosen(left_ref, BESIDE), chosen(right_ref, BESIDE)], axis=1
    ).astype(BF16)
    strips = jnp.concatenate([up_ref[0:STRIP], down_ref[0:STRIP]], axis=0)
    beside = jnp.concatenate(
        [field_ref[pl.ds(at(c, i, CELLS), 8), :] for c in range(COMPONENTS) for i in range(CELLS)], axis=0
    )
    restrict(strips, beside, across_ref, along_ref, basis_ref, sub_ref, coarse_ref)


def cross_multiply(rows_ref, column_ref, parts_ref):
    n_gy, k, width = rows_ref.shape
    rows = rows_ref[...].reshape(n_gy * k, width).astype(BF16)
    parts_ref[...] = matmul(rows, column_ref[...].reshape(width, LANES).astype(BF16)).reshape(parts_ref.shape)


def apply_inverse(inverse_hbm, sub_ref, patch_ref, inverse, sems):
    count = sems.shape[0]
    size = inverse.shape[0] // count
    parts = [pl.ds(i * size, size) for i in range(count)]
    chunks = [pltpu.make_async_copy(inverse_hbm.at[p], inverse.at[p], sems.at[i]) for i, p in enumerate(parts)]
    for chunk in chunks:
        chunk.start()
    for chunk, p in zip(chunks, parts):
        chunk.wait()
        patch_ref[p, :] = matmul(inverse[p, :], sub_ref[...])


def spread(depth, local_ref, basis_ref, parts_ref, across_ref, along_ref, field_ref, up_ref, down_ref, patch):
    coarse = jnp.sum(parts_ref[...], axis=0).astype(BF16)
    patch[...] = local_ref[...] + matmul(basis_ref[...], coarse, (0, 0))
    field_ref[...] = jnp.zeros_like(field_ref)
    across = matmul(across_ref[...], patch[OWN : OWN + 2 * MARGIN].astype(BF16))
    along = matmul(along_ref[...], patch[OWN + 2 * MARGIN :].astype(BF16))
    for c in range(COMPONENTS):
        for i in range(CELLS):
            n = c * CELLS + i
            field_ref[pl.ds(at(c, i), CELLS), :] = patch[n * CELLS : (n + 1) * CELLS]
            field_ref[pl.ds(at(c, i, CELLS), 8), :] = along[n * 8 : (n + 1) * 8]
        for layer in range(2):
            n = (c * 2 + layer) * CELLS
            field_ref[pl.ds(at(c, layer - 2), CELLS), :] = across[n : n + CELLS]
            field_ref[pl.ds(at(c, layer + CELLS), CELLS), :] = across[STRIP + n : STRIP + n + CELLS]
        part = part_of(depth)
        up_ref[c * part : (c + 1) * part] = field_ref[pl.ds(at(c, -2), part), :].astype(BF16)
        down_ref[c * part : (c + 1) * part] = field_ref[pl.ds(at(c, CELLS - depth), part), :].astype(BF16)


def add_across(depth, field_ref, up_ref, down_ref, out_ref, left_ref, right_ref, strip):
    part, layers = part_of(depth), depth + 2
    out_ref[...] = field_ref[...]
    for c in range(COMPONENTS):
        for first, ref in ((-depth, up_ref), (CELLS - 2, down_ref)):
            came = ref[c * part : (c + 1) * part].astype(F32)
            out_ref[pl.ds(at(c, first), layers * SIDE), :] += came[: layers * SIDE]
    for first, ref in ((-2, left_ref), (CELLS - depth, right_ref)):
        for c in range(COMPONENTS):
            for q in range(layers):
                strip[pl.ds(q * SIDE, SIDE), :] = out_ref[column_of(c, first + q, -ABOVE, SIDE), :]
            strip[layers * SIDE :] = jnp.zeros((part - layers * SIDE, LANES), F32)
            ref[c * part : (c + 1) * part] = strip[...].astype(BF16)


def add_along(depth, field_ref, left_ref, right_ref):
    part = part_of(depth)
    for c in range(COMPONENTS):
        for first, ref in ((-depth, left_ref), (CELLS - 2, right_ref)):
            came = ref[c * part : (c + 1) * part].astype(F32)
            for q in range(depth + 2):
                where = column_of(c, first + q, -ABOVE, SIDE)
                field_ref[where, :] = field_ref[where, :] + came[q * SIDE : (q + 1) * SIDE]


def operate_row(field, diagonal_ref, c, i):
    here = field(c, i)
    beside = field(c, i - 1) + field(c, i + 1) + pltpu.roll(here, 1, 0) + pltpu.roll(here, SIDE - 1, 0)
    return diagonal_ref[pl.ds(at(0, i), SIDE), :] * here - beside


def middle_pass(
    field_ref, left_ref, right_ref, values_ref, diagonal_ref, across_ref, along_ref, basis_ref,
    first_ref, sub_ref, coarse_ref, strips, beside,
):
    first_ref[...] = field_ref[...]
    add_along(3, first_ref, left_ref, right_ref)

    def field(c, i):
        return first_ref[pl.ds(at(c, i), SIDE), :]

    for c in range(COMPONENTS):
        for i in range(-2, CELLS + 2):
            middle = values_ref[pl.ds(at(c, i), SIDE), :] - operate_row(field, diagonal_ref, c, i)
            if 0 <= i < CELLS:
                n = c * CELLS + i
                sub_ref[n * CELLS : (n + 1) * CELLS] = middle[:CELLS].astype(BF16)
                beside[pl.ds(n * 8, 8), :] = middle[CELLS:]
            else:
                n = (c * 2 + (i + 2 if i < 0 else i - CELLS)) * CELLS + (0 if i < 0 else STRIP)
                strips[pl.ds(n, CELLS), :] = middle[:CELLS]
    restrict(strips[...], beside[...], across_ref, along_ref, basis_ref, sub_ref, coarse_ref)


def last_pass(field_ref, left_ref, right_ref, first_ref, values_ref, diagonal_ref, solution_ref, final_ref, total):
    total[...] = field_ref[...]
    add_along(1, total, left_ref, right_ref)
    total[...] += first_ref[...]

    def field(c, i):
        return total[pl.ds(at(c, i), SIDE), :]

    for c in range(COMPONENTS):
        for i in range(CELLS):
            rows = slice((c * CELLS + i) * CELLS, (c * CELLS + i + 1) * CELLS)
            solution_ref[rows] = total[pl.ds(at(c, i), CELLS), :]
            applied = operate_row(field, diagonal_ref, c, i)[:CELLS]
            final_ref[rows] = values_ref[pl.ds(at(c, i), CELLS), :] - applied


def trade(lower, upper, axis):
    count = lax.axis_size(axis)
    forward = [(i, i + 1) for i in range(count - 1)]
    backward = [(target, source) for source, target in forward]
    return lax.ppermute(upper, axis, forward), lax.ppermute(lower, axis, backward)


GX, GY = ("z", "core"), "gy"
FIRST, SECOND = "z", ("core", "gy")


def per_device(residual, stiffness, local_inverse, coarse_basis, coarse_rows, send_rows, partition_map):
    inverse, basis, lists = local_inverse[0, 0], coarse_basis[0, 0], send_rows[0, 0]
    k, order = coarse_rows.shape[2:]
    n_first, n_second = lax.axis_size(FIRST), lax.axis_size(SECOND)
    values = residual.reshape(OWN, LANES)
    swap = functools.partial(lax.all_to_all, split_axis=0, concat_axis=0, tiled=True)

    own, stiff = ((OWN, LANES), F32), (stiffness.shape, F32)
    edge = ((EDGE, LANES), F32)
    up, down, left, right = call(
        make_edges, [edge] * 4, values, stiffness, lists, fetched=3,
        scratch=[own, stiff, (lists.shape, jnp.int32)],
    )
    [crossing] = call(
        order_rows, [((n_second, k, n_first * k), F32)], coarse_rows[0, 0], partition_map, up, fetched=2,
        scratch=[((k, order), BF16), pltpu.SMEM(partition_map.shape, jnp.int32), ((order // LANES, k, LANES), F32)],
    )
    crossing = swap(crossing, SECOND)
    up, down = trade(up, down, GX)
    left, right = trade(left, right, GY)
    field = ((FIELD, LANES), F32)
    copies = ((n_first, k, LANES), F32)
    sub_kind = ((OWN + 4 * MARGIN, LANES), BF16)
    ambient, diagonal, across, along, sub, basis, coarse = call(
        start_pass,
        [
            field, ((PLANE, LANES), F32), ((2 * STRIP, 2 * MARGIN), BF16), ((BESIDE, 2 * MARGIN), BF16), sub_kind,
            (basis.shape, BF16), copies,
        ],
        values, stiffness, basis, up, down, left, right, fetched=3, scratch=[own, stiff],
    )

    def correct(depth, sub, coarse):
        patch = ((OWN + 4 * MARGIN, LANES), F32)
        [local] = call(
            apply_inverse, [patch], inverse, sub, fetched=1, copies=4, scratch=[(inverse.shape, BF16)],
            cost=(inverse.size * LANES * 2, inverse.size * 2),
        )
        [parts] = call(cross_multiply, [((n_second, k, LANES), F32)], crossing, swap(coarse, FIRST))
        part = ((COMPONENTS * part_of(depth), LANES), BF16)
        y, to_up, to_down = call(
            functools.partial(spread, depth), [field, part, part],
            local, basis, swap(parts, SECOND), across, along, scratch=[patch],
        )
        y, to_left, to_right = call(
            functools.partial(add_across, depth), [field, part, part], y, *trade(to_up, to_down, GX),
            scratch=[((part_of(depth), LANES), F32)],
        )
        return (y, *trade(to_left, to_right, GY))

    first, sub, coarse = call(
        middle_pass, [field, sub_kind, copies], *correct(3, sub, coarse), ambient, diagonal, across, along, basis,
        scratch=[((2 * STRIP, LANES), F32), ((BESIDE, LANES), F32)],
    )
    total, final = call(
        last_pass, [own, own], *correct(1, sub, coarse), first, ambient, diagonal, scratch=[field]
    )
    return total.reshape(residual.shape), final.reshape(residual.shape)


def solution(mesh):
    split = Mesh(mesh.devices.reshape(-1, 2, mesh.devices.shape[1]), ("z", "core", "gy"))
    cells = P(None, GX, GY, None)
    placed = (cells, P(GX, GY), *[P(GX, GY, None, None)] * 4, P())
    return jax.shard_map(per_device, mesh=split, in_specs=placed, out_specs=(cells, cells), check_vma=False)
```

```python
import functools

import jax
import jax.numpy as jnp
from jax import lax
from jax.experimental import pallas as pl
from jax.experimental.pallas import tpu as pltpu
from jax.sharding import Mesh
from jax.sharding import PartitionSpec as P

F32, BF16 = jnp.float32, jnp.bfloat16
COMPONENTS, CELLS, LANES = 3, 16, 128
OWN = COMPONENTS * CELLS * CELLS
MARGIN = 64
SIDE, ABOVE = 24, 4
PLANE = SIDE * SIDE
FIELD = COMPONENTS * PLANE
BESIDE = COMPONENTS * CELLS * 8
STRIP = COMPONENTS * 2 * CELLS
EDGE = STRIP + 2 * CELLS + 8
VMEM_BYTES = 8 * 2**20


def part_of(depth):
    return -(-(depth + 2) * SIDE // 16) * 16


def at(component, row, column=0):
    return component * PLANE + (row + ABOVE) * SIDE + column % SIDE


def column_of(component, column, first=0, count=CELLS):
    return pl.ds(at(component, first, column), count, stride=SIDE)


def matmul(a, b, contract=(1, 0)):
    return lax.dot_general(
        a, b, (((contract[0],), (contract[1],)), ((), ())), preferred_element_type=F32
    )


def call(kernel, outs, *args, scratch=(), fetched=0, copies=None, cost=None):
    vmem, hbm = pl.BlockSpec(memory_space=pltpu.VMEM), pl.BlockSpec(memory_space=pltpu.HBM)
    copies = [pltpu.SemaphoreType.DMA((copies or fetched,))] if fetched else []
    return pl.pallas_call(
        kernel,
        out_shape=[jax.ShapeDtypeStruct(shape, kind) for shape, kind in outs],
        in_specs=[hbm if i < fetched else vmem for i in range(len(args))],
        out_specs=[vmem] * len(outs),
        scratch_shapes=[*(pltpu.VMEM(*s) if isinstance(s, tuple) else s for s in scratch), *copies],
        compiler_params=pltpu.CompilerParams(vmem_limit_bytes=VMEM_BYTES),
        cost_estimate=pl.CostEstimate(flops=cost[0], bytes_accessed=cost[1], transcendentals=0) if cost else None,
    )(*(pltpu.with_memory_space_constraint(a, pltpu.HBM) if i < fetched else a for i, a in enumerate(args)))


def fetch(pairs, sems):
    copies = [pltpu.make_async_copy(source, target, sems.at[i]) for i, (source, target) in enumerate(pairs)]
    for copy in copies:
        copy.start()
    for copy in copies:
        copy.wait()


def order_rows(width, rows_hbm, places_hbm, basis_hbm, after_ref, out_ref, basis_ref, rows, places, tiles, sems):
    fetch([(rows_hbm, rows), (places_hbm, places), (basis_hbm, basis_ref)], sems)
    n_targets = out_ref.shape[0]
    for t in range(tiles.shape[0]):
        tiles[t] = rows[:, t * LANES : (t + 1) * LANES].astype(F32)
    slot = lax.broadcasted_iota(jnp.int32, (8, LANES), 1) // 8

    def one(target, carry):
        block = jnp.zeros((8, LANES), F32)
        for q in range(width // 8):
            place = places[q * n_targets + target]
            tile = tiles[lax.shift_right_logical(place, 4)]
            turned = pltpu.roll(tile, ((q + 16 - (place & 15)) & 15) * 8, 1)
            block = jnp.where(slot == q, turned, block)
        out_ref[target] = block
        return carry

    lax.fori_loop(0, n_targets, one, 0, unroll=8)


def make_edges(
    values_hbm, stiff_hbm, lists_hbm, values_ref, stiff_ref, up_ref, down_ref, left_ref, right_ref, lists_ref, sems
):
    fetch([(values_hbm, values_ref), (stiff_hbm, stiff_ref), (lists_hbm, lists_ref)], sems)
    lists = lists_ref[...]
    stiff = stiff_ref[...]
    turned = stiff.T
    component, i, j = lists >> 8, (lists >> 4) & 15, lists & 15
    codes = (
        component * 32 + i * 16 + j,
        component * 32 + (i - 14) * 16 + j,
        component * 128 + i * 8 + j,
        component * 128 + i * 8 + j - 8,
    )
    for side, ref in enumerate((up_ref, down_ref, left_ref, right_ref)):
        first = 0 if side in (0, 2) else CELLS - 2
        for c in range(COMPONENTS):
            for layer in range(2):
                if side < 2:
                    rows = pl.ds(c * 256 + (first + layer) * CELLS, CELLS)
                else:
                    rows = pl.ds(c * 256 + first + layer, CELLS, stride=CELLS)
                ref[pl.ds((c * 2 + layer) * CELLS, CELLS), :] = values_ref[rows, :]
        for layer in range(2):
            source = turned if side < 2 else stiff
            one = source[:, first + layer : first + layer + 1]
            ref[pl.ds(STRIP + layer * CELLS, CELLS), :] = jnp.broadcast_to(one, (CELLS, LANES))
        code = (codes[side][side : side + 1] + 1).astype(F32)
        ref[pl.ds(STRIP + 2 * CELLS, 8), 0:MARGIN] = jnp.broadcast_to(code, (8, MARGIN))


def restrict(strips, beside, across_ref, along_ref, basis_ref, sub_ref):
    sub_ref[OWN : OWN + 2 * MARGIN] = matmul(across_ref[...], strips.astype(BF16), (0, 0)).astype(BF16)
    sub_ref[OWN + 2 * MARGIN :] = matmul(along_ref[...], beside.astype(BF16), (0, 0)).astype(BF16)
    return matmul(basis_ref[...], sub_ref[...]).astype(BF16).astype(F32)


def start_pass(
    values_ref, stiff_ref, basis_ref, ordered_ref, up_ref, down_ref, left_ref, right_ref,
    field_ref, diagonal_ref, across_ref, along_ref, sub_ref, both_ref,
):
    turned = stiff_ref[...].T
    field_ref[...] = jnp.zeros_like(field_ref)
    diagonal_ref[...] = jnp.full(diagonal_ref.shape, 4.0, F32)
    for c in range(COMPONENTS):
        for i in range(CELLS):
            rows = values_ref[c * 256 + i * CELLS : c * 256 + (i + 1) * CELLS]
            field_ref[pl.ds(at(c, i), CELLS), :] = rows
            sub_ref[c * 256 + i * CELLS : c * 256 + (i + 1) * CELLS] = rows.astype(BF16)
        for layer in range(2):
            rows = pl.ds((c * 2 + layer) * CELLS, CELLS)
            field_ref[pl.ds(at(c, layer - 2), CELLS), :] = up_ref[rows, :]
            field_ref[pl.ds(at(c, layer + CELLS), CELLS), :] = down_ref[rows, :]
            field_ref[column_of(c, layer - 2), :] = left_ref[rows, :]
            field_ref[column_of(c, layer + CELLS), :] = right_ref[rows, :]
    for i in range(CELLS):
        diagonal_ref[pl.ds(at(0, i), CELLS), :] += jnp.broadcast_to(turned[:, i : i + 1], (CELLS, LANES))
    for layer in range(2):
        rows = pl.ds(STRIP + layer * CELLS, CELLS)
        diagonal_ref[pl.ds(at(0, layer - 2), CELLS), :] += up_ref[rows, :]
        diagonal_ref[pl.ds(at(0, layer + CELLS), CELLS), :] += down_ref[rows, :]
        diagonal_ref[column_of(0, layer - 2), :] += left_ref[rows, :]
        diagonal_ref[column_of(0, layer + CELLS), :] += right_ref[rows, :]

    def chosen(ref, rows):
        code = ref[STRIP + 2 * CELLS : STRIP + 2 * CELLS + 1, 0:MARGIN]
        spot = lax.broadcasted_iota(jnp.int32, (rows, MARGIN), 0).astype(F32) + 1.0
        return jnp.where(spot == code, 1.0, 0.0)

    none = jnp.zeros((STRIP, MARGIN), F32)
    across_ref[...] = jnp.concatenate(
        [
            jnp.concatenate([chosen(up_ref, STRIP), none], axis=1),
            jnp.concatenate([none, chosen(down_ref, STRIP)], axis=1),
        ],
        axis=0,
    ).astype(BF16)
    along_ref[...] = jnp.concatenate(
        [chosen(left_ref, BESIDE), chosen(right_ref, BESIDE)], axis=1
    ).astype(BF16)
    strips = jnp.concatenate([up_ref[0:STRIP], down_ref[0:STRIP]], axis=0)
    beside = jnp.concatenate(
        [field_ref[pl.ds(at(c, i, CELLS), 8), :] for c in range(COMPONENTS) for i in range(CELLS)], axis=0
    )
    coarse = restrict(strips, beside, across_ref, along_ref, basis_ref, sub_ref)
    for target in range(both_ref.shape[0]):
        both_ref[target] = jnp.concatenate([ordered_ref[target], coarse], axis=0).astype(BF16)


def cross_first(both_ref, rows_ref, parts_ref):
    n, k = both_ref.shape[0], both_ref.shape[1] // 2
    both = both_ref[...].astype(F32)
    rows_ref[...] = both[:, :k].reshape(n * k, LANES).astype(BF16)
    parts = matmul(rows_ref[...], both[:, k:].reshape(n * k, LANES).astype(BF16), (0, 0))
    parts_ref[...] = parts[: parts_ref.shape[0] * k].reshape(parts_ref.shape)


def cross_second(rows_ref, column_ref, parts_ref):
    n, k = column_ref.shape[:2]
    parts = matmul(rows_ref[...], column_ref[...].reshape(n * k, LANES).astype(BF16), (0, 0))
    parts_ref[...] = parts[: parts_ref.shape[0] * k].reshape(parts_ref.shape)


def apply_inverse(inverse_hbm, sub_ref, patch_ref, inverse, sems):
    count = sems.shape[0]
    size = inverse.shape[0] // count
    parts = [pl.ds(i * size, size) for i in range(count)]
    chunks = [pltpu.make_async_copy(inverse_hbm.at[p], inverse.at[p], sems.at[i]) for i, p in enumerate(parts)]
    for chunk in chunks:
        chunk.start()
    for chunk, p in zip(chunks, parts):
        chunk.wait()
        patch_ref[p, :] = matmul(inverse[p, :], sub_ref[...])


def spread(depth, local_ref, basis_ref, parts_ref, across_ref, along_ref, field_ref, up_ref, down_ref, patch):
    coarse = jnp.sum(parts_ref[...], axis=0).astype(BF16)
    patch[...] = local_ref[...] + matmul(basis_ref[...], coarse, (0, 0))
    field_ref[...] = jnp.zeros_like(field_ref)
    across = matmul(across_ref[...], patch[OWN : OWN + 2 * MARGIN].astype(BF16))
    along = matmul(along_ref[...], patch[OWN + 2 * MARGIN :].astype(BF16))
    for c in range(COMPONENTS):
        for i in range(CELLS):
            n = c * CELLS + i
            field_ref[pl.ds(at(c, i), CELLS), :] = patch[n * CELLS : (n + 1) * CELLS]
            field_ref[pl.ds(at(c, i, CELLS), 8), :] = along[n * 8 : (n + 1) * 8]
        for layer in range(2):
            n = (c * 2 + layer) * CELLS
            field_ref[pl.ds(at(c, layer - 2), CELLS), :] = across[n : n + CELLS]
            field_ref[pl.ds(at(c, layer + CELLS), CELLS), :] = across[STRIP + n : STRIP + n + CELLS]
        part = part_of(depth)
        up_ref[c * part : (c + 1) * part] = field_ref[pl.ds(at(c, -2), part), :].astype(BF16)
        down_ref[c * part : (c + 1) * part] = field_ref[pl.ds(at(c, CELLS - depth), part), :].astype(BF16)


def add_across(depth, field_ref, up_ref, down_ref, out_ref, left_ref, right_ref, strip):
    part, layers = part_of(depth), depth + 2
    out_ref[...] = field_ref[...]
    for c in range(COMPONENTS):
        for first, ref in ((-depth, up_ref), (CELLS - 2, down_ref)):
            came = ref[c * part : (c + 1) * part].astype(F32)
            out_ref[pl.ds(at(c, first), layers * SIDE), :] += came[: layers * SIDE]
    for first, ref in ((-2, left_ref), (CELLS - depth, right_ref)):
        for c in range(COMPONENTS):
            for q in range(layers):
                strip[pl.ds(q * SIDE, SIDE), :] = out_ref[column_of(c, first + q, -ABOVE, SIDE), :]
            strip[layers * SIDE :] = jnp.zeros((part - layers * SIDE, LANES), F32)
            ref[c * part : (c + 1) * part] = strip[...].astype(BF16)


def add_along(depth, field_ref, left_ref, right_ref):
    part = part_of(depth)
    for c in range(COMPONENTS):
        for first, ref in ((-depth, left_ref), (CELLS - 2, right_ref)):
            came = ref[c * part : (c + 1) * part].astype(F32)
            for q in range(depth + 2):
                where = column_of(c, first + q, -ABOVE, SIDE)
                field_ref[where, :] = field_ref[where, :] + came[q * SIDE : (q + 1) * SIDE]


def operate_row(field, diagonal_ref, c, i):
    here = field(c, i)
    beside = field(c, i - 1) + field(c, i + 1) + pltpu.roll(here, 1, 0) + pltpu.roll(here, SIDE - 1, 0)
    return diagonal_ref[pl.ds(at(0, i), SIDE), :] * here - beside


def middle_pass(
    field_ref, left_ref, right_ref, values_ref, diagonal_ref, across_ref, along_ref, basis_ref,
    first_ref, sub_ref, coarse_ref, strips, beside,
):
    first_ref[...] = field_ref[...]
    add_along(3, first_ref, left_ref, right_ref)

    def field(c, i):
        return first_ref[pl.ds(at(c, i), SIDE), :]

    for c in range(COMPONENTS):
        for i in range(-2, CELLS + 2):
            middle = values_ref[pl.ds(at(c, i), SIDE), :] - operate_row(field, diagonal_ref, c, i)
            if 0 <= i < CELLS:
                n = c * CELLS + i
                sub_ref[n * CELLS : (n + 1) * CELLS] = middle[:CELLS].astype(BF16)
                beside[pl.ds(n * 8, 8), :] = middle[CELLS:]
            else:
                n = (c * 2 + (i + 2 if i < 0 else i - CELLS)) * CELLS + (0 if i < 0 else STRIP)
                strips[pl.ds(n, CELLS), :] = middle[:CELLS]
    coarse = restrict(strips[...], beside[...], across_ref, along_ref, basis_ref, sub_ref)
    for target in range(coarse_ref.shape[0]):
        coarse_ref[target] = coarse


def last_pass(field_ref, left_ref, right_ref, first_ref, values_ref, diagonal_ref, solution_ref, final_ref, total):
    total[...] = field_ref[...]
    add_along(1, total, left_ref, right_ref)
    total[...] += first_ref[...]

    def field(c, i):
        return total[pl.ds(at(c, i), SIDE), :]

    for c in range(COMPONENTS):
        for i in range(CELLS):
            rows = slice((c * CELLS + i) * CELLS, (c * CELLS + i + 1) * CELLS)
            solution_ref[rows] = total[pl.ds(at(c, i), CELLS), :]
            applied = operate_row(field, diagonal_ref, c, i)[:CELLS]
            final_ref[rows] = values_ref[pl.ds(at(c, i), CELLS), :] - applied


def trade(lower, upper, axis):
    count = lax.axis_size(axis)
    forward = [(i, i + 1) for i in range(count - 1)]
    backward = [(target, source) for source, target in forward]
    return lax.ppermute(upper, axis, forward), lax.ppermute(lower, axis, backward)


GX, GY = ("z", "core"), "gy"
FIRST, SECOND = ("core", "gy"), "z"


def per_device(residual, stiffness, local_inverse, coarse_basis, coarse_rows, send_rows, partition_map):
    inverse, basis, lists = local_inverse[0, 0], coarse_basis[0, 0], send_rows[0, 0]
    k, order = coarse_rows.shape[2:]
    n_first, n_second = lax.axis_size(FIRST), lax.axis_size(SECOND)
    values = residual.reshape(OWN, LANES)
    swap = functools.partial(lax.all_to_all, split_axis=0, concat_axis=0, tiled=True)

    own, field, edge = ((OWN, LANES), F32), ((FIELD, LANES), F32), ((EDGE, LANES), F32)
    sub_kind, patch = ((OWN + 4 * MARGIN, LANES), BF16), ((OWN + 4 * MARGIN, LANES), F32)
    copies, sums = ((n_first, k, LANES), F32), ((n_second, k, LANES), F32)
    values, stiffness, up, down, left, right = call(
        make_edges, [own, (stiffness.shape, F32), *[edge] * 4], values, stiffness, lists, fetched=3,
        scratch=[(lists.shape, jnp.int32)],
    )
    ordered, basis = call(
        functools.partial(order_rows, n_second * k), [copies, (basis.shape, BF16)],
        coarse_rows[0, 0], partition_map, basis, up, fetched=3,
        scratch=[((k, order), BF16), pltpu.SMEM(partition_map.shape, jnp.int32), ((order // LANES, k, LANES), F32)],
    )
    up, down = trade(up, down, GX)
    left, right = trade(left, right, GY)
    ambient, diagonal, across, along, sub, both = call(
        start_pass,
        [
            field, ((PLANE, LANES), F32), ((2 * STRIP, 2 * MARGIN), BF16), ((BESIDE, 2 * MARGIN), BF16), sub_kind,
            ((n_first, 2 * k, LANES), BF16),
        ],
        values, stiffness, basis, ordered, up, down, left, right,
    )

    def correct(depth, sub, parts):
        part = ((COMPONENTS * part_of(depth), LANES), BF16)
        [local] = call(
            apply_inverse, [patch], inverse, sub, fetched=1, copies=4, scratch=[(inverse.shape, BF16)],
            cost=(inverse.size * LANES * 2, inverse.size * 2),
        )
        y, to_up, to_down = call(
            functools.partial(spread, depth), [field, part, part],
            local, basis, swap(parts, SECOND), across, along, scratch=[patch],
        )
        y, to_left, to_right = call(
            functools.partial(add_across, depth), [field, part, part], y, *trade(to_up, to_down, GX),
            scratch=[((part_of(depth), LANES), F32)],
        )
        return (y, *trade(to_left, to_right, GY))

    crossing, parts = call(cross_first, [((n_first * k, LANES), BF16), sums], swap(both, FIRST))
    first, sub, coarse = call(
        middle_pass, [field, sub_kind, copies], *correct(3, sub, parts), ambient, diagonal, across, along, basis,
        scratch=[((2 * STRIP, LANES), F32), ((BESIDE, LANES), F32)],
    )
    [parts] = call(cross_second, [sums], crossing, swap(coarse, FIRST))
    total, final = call(
        last_pass, [own, own], *correct(1, sub, parts), first, ambient, diagonal, scratch=[field]
    )
    return total.reshape(residual.shape), final.reshape(residual.shape)


def solution(mesh):
    split = Mesh(mesh.devices.reshape(-1, 2, mesh.devices.shape[1]), ("z", "core", "gy"))
    cells = P(None, GX, GY, None)
    placed = (cells, P(GX, GY), *[P(GX, GY, None, None)] * 4, P())
    return jax.shard_map(per_device, mesh=split, in_specs=placed, out_specs=(cells, cells), check_vma=False)
```

```python
import functools

import jax
import jax.numpy as jnp
from jax import lax
from jax.experimental import pallas as pl
from jax.experimental.pallas import tpu as pltpu
from jax.sharding import Mesh
from jax.sharding import PartitionSpec as P

F32, BF16 = jnp.float32, jnp.bfloat16
COMPONENTS, CELLS, LANES = 3, 16, 128
OWN = COMPONENTS * CELLS * CELLS
MARGIN = 64
SIDE, ABOVE = 24, 4
PLANE = SIDE * SIDE
FIELD = COMPONENTS * PLANE
BESIDE = COMPONENTS * CELLS * 8
STRIP = COMPONENTS * 2 * CELLS
EDGE = STRIP + 2 * CELLS + 8
VMEM_BYTES = 8 * 2**20


def part_of(depth):
    return -(-(depth + 2) * SIDE // 16) * 16


def at(component, row, column=0):
    return component * PLANE + (row + ABOVE) * SIDE + column % SIDE


def column_of(component, column, first=0, count=CELLS):
    return pl.ds(at(component, first, column), count, stride=SIDE)


def matmul(a, b, contract=(1, 0)):
    return lax.dot_general(
        a, b, (((contract[0],), (contract[1],)), ((), ())), preferred_element_type=F32
    )


def call(kernel, outs, *args, scratch=(), fetched=0, copies=None, cost=None):
    vmem, hbm = pl.BlockSpec(memory_space=pltpu.VMEM), pl.BlockSpec(memory_space=pltpu.HBM)
    copies = [pltpu.SemaphoreType.DMA((copies or fetched,))] if fetched else []
    return pl.pallas_call(
        kernel,
        out_shape=[jax.ShapeDtypeStruct(shape, kind) for shape, kind in outs],
        in_specs=[hbm if i < fetched else vmem for i in range(len(args))],
        out_specs=[vmem] * len(outs),
        scratch_shapes=[*(pltpu.VMEM(*s) if isinstance(s, tuple) else s for s in scratch), *copies],
        compiler_params=pltpu.CompilerParams(vmem_limit_bytes=VMEM_BYTES),
        cost_estimate=pl.CostEstimate(flops=cost[0], bytes_accessed=cost[1], transcendentals=0) if cost else None,
    )(*(pltpu.with_memory_space_constraint(a, pltpu.HBM) if i < fetched else a for i, a in enumerate(args)))


def fetch(pairs, sems):
    copies = [pltpu.make_async_copy(source, target, sems.at[i]) for i, (source, target) in enumerate(pairs)]
    for copy in copies:
        copy.start()
    for copy in copies:
        copy.wait()


def by_chip(lower, upper):
    second = lax.axis_index("core") == 1
    return jnp.where(second, lower, upper), jnp.where(second, upper, lower)


def by_side(inner, outer):
    second = lax.axis_index("core") == 1
    return jnp.where(second, inner, outer), jnp.where(second, outer, inner)


def order_rows(width, rows_hbm, places_hbm, basis_hbm, after_ref, out_ref, basis_ref, rows, places, tiles, sems):
    fetch([(rows_hbm, rows), (places_hbm, places), (basis_hbm, basis_ref)], sems)
    n_targets = out_ref.shape[0]
    for t in range(tiles.shape[0]):
        tiles[t] = rows[:, t * LANES : (t + 1) * LANES].astype(F32)
    slot = lax.broadcasted_iota(jnp.int32, (8, LANES), 1) // 8

    def one(target, carry):
        block = jnp.zeros((8, LANES), F32)
        for q in range(width // 8):
            place = places[q * n_targets + target]
            tile = tiles[lax.shift_right_logical(place, 4)]
            turned = pltpu.roll(tile, ((q + 16 - (place & 15)) & 15) * 8, 1)
            block = jnp.where(slot == q, turned, block)
        out_ref[target] = block
        return carry

    lax.fori_loop(0, n_targets, one, 0, unroll=8)


def make_edges(
    values_hbm, stiff_hbm, lists_hbm, values_ref, stiff_ref, inner_ref, outer_ref, left_ref, right_ref,
    lists_ref, up_ref, down_ref, sems,
):
    fetch([(values_hbm, values_ref), (stiff_hbm, stiff_ref), (lists_hbm, lists_ref)], sems)
    lists = lists_ref[...]
    stiff = stiff_ref[...]
    turned = stiff.T
    component, i, j = lists >> 8, (lists >> 4) & 15, lists & 15
    codes = (
        component * 32 + i * 16 + j,
        component * 32 + (i - 14) * 16 + j,
        component * 128 + i * 8 + j,
        component * 128 + i * 8 + j - 8,
    )
    for side, ref in enumerate((up_ref, down_ref, left_ref, right_ref)):
        first = 0 if side in (0, 2) else CELLS - 2
        for c in range(COMPONENTS):
            for layer in range(2):
                if side < 2:
                    rows = pl.ds(c * 256 + (first + layer) * CELLS, CELLS)
                else:
                    rows = pl.ds(c * 256 + first + layer, CELLS, stride=CELLS)
                ref[pl.ds((c * 2 + layer) * CELLS, CELLS), :] = values_ref[rows, :]
        for layer in range(2):
            source = turned if side < 2 else stiff
            one = source[:, first + layer : first + layer + 1]
            ref[pl.ds(STRIP + layer * CELLS, CELLS), :] = jnp.broadcast_to(one, (CELLS, LANES))
        code = (codes[side][side : side + 1] + 1).astype(F32)
        code = jnp.concatenate([code, jnp.zeros((1, LANES - MARGIN), F32)], axis=1)
        ref[pl.ds(STRIP + 2 * CELLS, 8), :] = jnp.broadcast_to(code, (8, LANES))
    inner_ref[...], outer_ref[...] = by_chip(up_ref[...], down_ref[...])


def restrict(strips, beside, across_ref, along_ref, basis_ref, sub_ref):
    sub_ref[OWN : OWN + 2 * MARGIN] = matmul(across_ref[...], strips.astype(BF16), (0, 0)).astype(BF16)
    sub_ref[OWN + 2 * MARGIN :] = matmul(along_ref[...], beside.astype(BF16), (0, 0)).astype(BF16)
    return matmul(basis_ref[...], sub_ref[...]).astype(BF16).astype(F32)


def start_pass(
    values_ref, stiff_ref, basis_ref, ordered_ref, inner_ref, outer_ref, left_ref, right_ref,
    field_ref, diagonal_ref, across_ref, along_ref, sub_ref, both_ref, up_ref, down_ref,
):
    up_ref[...], down_ref[...] = by_side(inner_ref[...], outer_ref[...])
    turned = stiff_ref[...].T
    field_ref[...] = jnp.zeros_like(field_ref)
    diagonal_ref[...] = jnp.full(diagonal_ref.shape, 4.0, F32)
    for c in range(COMPONENTS):
        for i in range(CELLS):
            rows = values_ref[c * 256 + i * CELLS : c * 256 + (i + 1) * CELLS]
            field_ref[pl.ds(at(c, i), CELLS), :] = rows
            sub_ref[c * 256 + i * CELLS : c * 256 + (i + 1) * CELLS] = rows.astype(BF16)
        for layer in range(2):
            rows = pl.ds((c * 2 + layer) * CELLS, CELLS)
            field_ref[pl.ds(at(c, layer - 2), CELLS), :] = up_ref[rows, :]
            field_ref[pl.ds(at(c, layer + CELLS), CELLS), :] = down_ref[rows, :]
            field_ref[column_of(c, layer - 2), :] = left_ref[rows, :]
            field_ref[column_of(c, layer + CELLS), :] = right_ref[rows, :]
    for i in range(CELLS):
        diagonal_ref[pl.ds(at(0, i), CELLS), :] += jnp.broadcast_to(turned[:, i : i + 1], (CELLS, LANES))
    for layer in range(2):
        rows = pl.ds(STRIP + layer * CELLS, CELLS)
        diagonal_ref[pl.ds(at(0, layer - 2), CELLS), :] += up_ref[rows, :]
        diagonal_ref[pl.ds(at(0, layer + CELLS), CELLS), :] += down_ref[rows, :]
        diagonal_ref[column_of(0, layer - 2), :] += left_ref[rows, :]
        diagonal_ref[column_of(0, layer + CELLS), :] += right_ref[rows, :]

    def chosen(ref, rows):
        code = ref[STRIP + 2 * CELLS : STRIP + 2 * CELLS + 1, 0:MARGIN]
        spot = lax.broadcasted_iota(jnp.int32, (rows, MARGIN), 0).astype(F32) + 1.0
        return jnp.where(spot == code, 1.0, 0.0)

    none = jnp.zeros((STRIP, MARGIN), F32)
    across_ref[...] = jnp.concatenate(
        [
            jnp.concatenate([chosen(up_ref, STRIP), none], axis=1),
            jnp.concatenate([none, chosen(down_ref, STRIP)], axis=1),
        ],
        axis=0,
    ).astype(BF16)
    along_ref[...] = jnp.concatenate(
        [chosen(left_ref, BESIDE), chosen(right_ref, BESIDE)], axis=1
    ).astype(BF16)
    strips = jnp.concatenate([up_ref[0:STRIP], down_ref[0:STRIP]], axis=0)
    beside = jnp.concatenate(
        [field_ref[pl.ds(at(c, i, CELLS), 8), :] for c in range(COMPONENTS) for i in range(CELLS)], axis=0
    )
    coarse = restrict(strips, beside, across_ref, along_ref, basis_ref, sub_ref)
    for target in range(both_ref.shape[0]):
        both_ref[target] = jnp.concatenate([ordered_ref[target], coarse], axis=0).astype(BF16)


def cross_first(both_ref, rows_ref, parts_ref):
    n, k = both_ref.shape[0], both_ref.shape[1] // 2
    both = both_ref[...].astype(F32)
    rows_ref[...] = both[:, :k].reshape(n * k, LANES).astype(BF16)
    parts = matmul(rows_ref[...], both[:, k:].reshape(n * k, LANES).astype(BF16), (0, 0))
    parts_ref[...] = parts[: parts_ref.shape[0] * k].reshape(parts_ref.shape)


def cross_second(rows_ref, column_ref, parts_ref):
    n, k = column_ref.shape[:2]
    parts = matmul(rows_ref[...], column_ref[...].reshape(n * k, LANES).astype(BF16), (0, 0))
    parts_ref[...] = parts[: parts_ref.shape[0] * k].reshape(parts_ref.shape)


def apply_inverse(inverse_hbm, sub_ref, patch_ref, inverse, sems):
    count = sems.shape[0]
    size = inverse.shape[0] // count
    parts = [pl.ds(i * size, size) for i in range(count)]
    chunks = [pltpu.make_async_copy(inverse_hbm.at[p], inverse.at[p], sems.at[i]) for i, p in enumerate(parts)]
    for chunk in chunks:
        chunk.start()
    for chunk, p in zip(chunks, parts):
        chunk.wait()
        patch_ref[p, :] = matmul(inverse[p, :], sub_ref[...])


def spread(depth, local_ref, basis_ref, parts_ref, across_ref, along_ref, field_ref, inner_ref, outer_ref, patch):
    coarse = jnp.sum(parts_ref[...], axis=0).astype(BF16)
    patch[...] = local_ref[...] + matmul(basis_ref[...], coarse, (0, 0))
    field_ref[...] = jnp.zeros_like(field_ref)
    across = matmul(across_ref[...], patch[OWN : OWN + 2 * MARGIN].astype(BF16))
    along = matmul(along_ref[...], patch[OWN + 2 * MARGIN :].astype(BF16))
    for c in range(COMPONENTS):
        for i in range(CELLS):
            n = c * CELLS + i
            field_ref[pl.ds(at(c, i), CELLS), :] = patch[n * CELLS : (n + 1) * CELLS]
            field_ref[pl.ds(at(c, i, CELLS), 8), :] = along[n * 8 : (n + 1) * 8]
        for layer in range(2):
            n = (c * 2 + layer) * CELLS
            field_ref[pl.ds(at(c, layer - 2), CELLS), :] = across[n : n + CELLS]
            field_ref[pl.ds(at(c, layer + CELLS), CELLS), :] = across[STRIP + n : STRIP + n + CELLS]
        part = part_of(depth)
        inner, outer = by_chip(field_ref[pl.ds(at(c, -2), part), :], field_ref[pl.ds(at(c, CELLS - depth), part), :])
        inner_ref[c * part : (c + 1) * part] = inner.astype(BF16)
        outer_ref[c * part : (c + 1) * part] = outer.astype(BF16)


def add_across(depth, field_ref, inner_ref, outer_ref, out_ref, left_ref, right_ref, strip):
    part, layers = part_of(depth), depth + 2
    out_ref[...] = field_ref[...]
    for c in range(COMPONENTS):
        rows = slice(c * part, (c + 1) * part)
        up, down = by_side(inner_ref[rows].astype(F32), outer_ref[rows].astype(F32))
        for first, came in ((-depth, up), (CELLS - 2, down)):
            out_ref[pl.ds(at(c, first), layers * SIDE), :] += came[: layers * SIDE]
    for first, ref in ((-2, left_ref), (CELLS - depth, right_ref)):
        for c in range(COMPONENTS):
            for q in range(layers):
                strip[pl.ds(q * SIDE, SIDE), :] = out_ref[column_of(c, first + q, -ABOVE, SIDE), :]
            strip[layers * SIDE :] = jnp.zeros((part - layers * SIDE, LANES), F32)
            ref[c * part : (c + 1) * part] = strip[...].astype(BF16)


def add_along(depth, field_ref, left_ref, right_ref):
    part = part_of(depth)
    for c in range(COMPONENTS):
        for first, ref in ((-depth, left_ref), (CELLS - 2, right_ref)):
            came = ref[c * part : (c + 1) * part].astype(F32)
            for q in range(depth + 2):
                where = column_of(c, first + q, -ABOVE, SIDE)
                field_ref[where, :] = field_ref[where, :] + came[q * SIDE : (q + 1) * SIDE]


def operate_row(field, diagonal_ref, c, i):
    here = field(c, i)
    beside = field(c, i - 1) + field(c, i + 1) + pltpu.roll(here, 1, 0) + pltpu.roll(here, SIDE - 1, 0)
    return diagonal_ref[pl.ds(at(0, i), SIDE), :] * here - beside


def middle_pass(
    field_ref, left_ref, right_ref, values_ref, diagonal_ref, across_ref, along_ref, basis_ref,
    first_ref, sub_ref, coarse_ref, strips, beside,
):
    first_ref[...] = field_ref[...]
    add_along(3, first_ref, left_ref, right_ref)

    def field(c, i):
        return first_ref[pl.ds(at(c, i), SIDE), :]

    for c in range(COMPONENTS):
        for i in range(-2, CELLS + 2):
            middle = values_ref[pl.ds(at(c, i), SIDE), :] - operate_row(field, diagonal_ref, c, i)
            if 0 <= i < CELLS:
                n = c * CELLS + i
                sub_ref[n * CELLS : (n + 1) * CELLS] = middle[:CELLS].astype(BF16)
                beside[pl.ds(n * 8, 8), :] = middle[CELLS:]
            else:
                n = (c * 2 + (i + 2 if i < 0 else i - CELLS)) * CELLS + (0 if i < 0 else STRIP)
                strips[pl.ds(n, CELLS), :] = middle[:CELLS]
    coarse = restrict(strips[...], beside[...], across_ref, along_ref, basis_ref, sub_ref)
    for target in range(coarse_ref.shape[0]):
        coarse_ref[target] = coarse


def last_pass(field_ref, left_ref, right_ref, first_ref, values_ref, diagonal_ref, solution_ref, final_ref, total):
    total[...] = field_ref[...]
    add_along(1, total, left_ref, right_ref)
    total[...] += first_ref[...]

    def field(c, i):
        return total[pl.ds(at(c, i), SIDE), :]

    for c in range(COMPONENTS):
        for i in range(CELLS):
            rows = slice((c * CELLS + i) * CELLS, (c * CELLS + i + 1) * CELLS)
            solution_ref[rows] = total[pl.ds(at(c, i), CELLS), :]
            applied = operate_row(field, diagonal_ref, c, i)[:CELLS]
            final_ref[rows] = values_ref[pl.ds(at(c, i), CELLS), :] - applied


def trade(lower, upper, axis):
    count = lax.axis_size(axis)
    forward = [(i, i + 1) for i in range(count - 1)]
    backward = [(target, source) for source, target in forward]
    return lax.ppermute(upper, axis, forward), lax.ppermute(lower, axis, backward)


def trade_by_chip(inner, outer):
    count = lax.axis_size(GX)

    def swap(message, start):
        pairs = [(i, i + 1) for i in range(start, count - 1, 2)]
        return lax.ppermute(message, GX, pairs + [(target, source) for source, target in pairs])

    outer = swap(outer, 1)
    return swap(inner, 0), outer


GX, GY = ("z", "core"), "gy"
FIRST, SECOND = ("core", "gy"), "z"


def per_device(residual, stiffness, local_inverse, coarse_basis, coarse_rows, send_rows, partition_map):
    inverse, basis, lists = local_inverse[0, 0], coarse_basis[0, 0], send_rows[0, 0]
    k, order = coarse_rows.shape[2:]
    n_first, n_second = lax.axis_size(FIRST), lax.axis_size(SECOND)
    values = residual.reshape(OWN, LANES)
    swap = functools.partial(lax.all_to_all, split_axis=0, concat_axis=0, tiled=True)

    own, field, edge = ((OWN, LANES), F32), ((FIELD, LANES), F32), ((EDGE, LANES), F32)
    sub_kind, patch = ((OWN + 4 * MARGIN, LANES), BF16), ((OWN + 4 * MARGIN, LANES), F32)
    copies, sums = ((n_first, k, LANES), F32), ((n_second, k, LANES), F32)
    values, stiffness, inner, outer, left, right = call(
        make_edges, [own, (stiffness.shape, F32), *[edge] * 4], values, stiffness, lists, fetched=3,
        scratch=[(lists.shape, jnp.int32), edge, edge],
    )
    ordered, basis = call(
        functools.partial(order_rows, n_second * k), [copies, (basis.shape, BF16)],
        coarse_rows[0, 0], partition_map, basis, inner, fetched=3,
        scratch=[((k, order), BF16), pltpu.SMEM(partition_map.shape, jnp.int32), ((order // LANES, k, LANES), F32)],
    )
    inner, outer = trade_by_chip(inner, outer)
    left, right = trade(left, right, GY)
    ambient, diagonal, across, along, sub, both = call(
        start_pass,
        [
            field, ((PLANE, LANES), F32), ((2 * STRIP, 2 * MARGIN), BF16), ((BESIDE, 2 * MARGIN), BF16), sub_kind,
            ((n_first, 2 * k, LANES), BF16),
        ],
        values, stiffness, basis, ordered, inner, outer, left, right, scratch=[edge, edge],
    )

    def correct(depth, sub, parts):
        part = ((COMPONENTS * part_of(depth), LANES), BF16)
        [local] = call(
            apply_inverse, [patch], inverse, sub, fetched=1, copies=4, scratch=[(inverse.shape, BF16)],
            cost=(inverse.size * LANES * 2, inverse.size * 2),
        )
        y, inner, outer = call(
            functools.partial(spread, depth), [field, part, part],
            local, basis, swap(parts, SECOND), across, along, scratch=[patch],
        )
        y, to_left, to_right = call(
            functools.partial(add_across, depth), [field, part, part], y, *trade_by_chip(inner, outer),
            scratch=[((part_of(depth), LANES), F32)],
        )
        return (y, *trade(to_left, to_right, GY))

    crossing, parts = call(cross_first, [((n_first * k, LANES), BF16), sums], swap(both, FIRST))
    first, sub, coarse = call(
        middle_pass, [field, sub_kind, copies], *correct(3, sub, parts), ambient, diagonal, across, along, basis,
        scratch=[((2 * STRIP, LANES), F32), ((BESIDE, LANES), F32)],
    )
    [parts] = call(cross_second, [sums], crossing, swap(coarse, FIRST))
    total, final = call(
        last_pass, [own, own], *correct(1, sub, parts), first, ambient, diagonal, scratch=[field]
    )
    return total.reshape(residual.shape), final.reshape(residual.shape)


def solution(mesh):
    split = Mesh(mesh.devices.reshape(-1, 2, mesh.devices.shape[1]), ("z", "core", "gy"))
    cells = P(None, GX, GY, None)
    placed = (cells, P(GX, GY), *[P(GX, GY, None, None)] * 4, P())
    return jax.shard_map(per_device, mesh=split, in_specs=placed, out_specs=(cells, cells), check_vma=False)
```

```python
import functools

import jax
import jax.numpy as jnp
from jax import lax
from jax.experimental import pallas as pl
from jax.experimental.pallas import tpu as pltpu
from jax.sharding import Mesh
from jax.sharding import PartitionSpec as P

F32, BF16 = jnp.float32, jnp.bfloat16
COMPONENTS, CELLS, LANES = 3, 16, 128
OWN = COMPONENTS * CELLS * CELLS
MARGIN = 64
SIDE, ABOVE = 24, 4
PLANE = SIDE * SIDE
FIELD = COMPONENTS * PLANE
BESIDE = COMPONENTS * CELLS * 8
STRIP = COMPONENTS * 2 * CELLS
EDGE = STRIP + 2 * CELLS + 8
VMEM_BYTES = 8 * 2**20


def part_of(depth):
    return -(-(depth + 2) * SIDE // 16) * 16


def at(component, row, column=0):
    return component * PLANE + (row + ABOVE) * SIDE + column % SIDE


def column_of(component, column, first=0, count=CELLS):
    return pl.ds(at(component, first, column), count, stride=SIDE)


def matmul(a, b, contract=(1, 0)):
    return lax.dot_general(
        a, b, (((contract[0],), (contract[1],)), ((), ())), preferred_element_type=F32
    )


def call(kernel, outs, *args, scratch=(), fetched=0, copies=None, cost=None):
    vmem, hbm = pl.BlockSpec(memory_space=pltpu.VMEM), pl.BlockSpec(memory_space=pltpu.HBM)
    copies = [pltpu.SemaphoreType.DMA((copies or fetched,))] if fetched else []
    return pl.pallas_call(
        kernel,
        out_shape=[jax.ShapeDtypeStruct(shape, kind) for shape, kind in outs],
        in_specs=[hbm if i < fetched else vmem for i in range(len(args))],
        out_specs=[vmem] * len(outs),
        scratch_shapes=[*(pltpu.VMEM(*s) if isinstance(s, tuple) else s for s in scratch), *copies],
        compiler_params=pltpu.CompilerParams(vmem_limit_bytes=VMEM_BYTES),
        cost_estimate=pl.CostEstimate(flops=cost[0], bytes_accessed=cost[1], transcendentals=0) if cost else None,
    )(*(pltpu.with_memory_space_constraint(a, pltpu.HBM) if i < fetched else a for i, a in enumerate(args)))


def fetch(pairs, sems):
    copies = [pltpu.make_async_copy(source, target, sems.at[i]) for i, (source, target) in enumerate(pairs)]
    for copy in copies:
        copy.start()
    for copy in copies:
        copy.wait()


def by_chip(lower, upper):
    second = lax.axis_index("core") == 1
    return jnp.where(second, lower, upper), jnp.where(second, upper, lower)


def by_side(inner, outer):
    second = lax.axis_index("core") == 1
    return jnp.where(second, inner, outer), jnp.where(second, outer, inner)


def order_rows(width, rows_hbm, places_hbm, basis_hbm, after_ref, out_ref, basis_ref, rows, places, tiles, sems):
    fetch([(rows_hbm, rows), (places_hbm, places), (basis_hbm, basis_ref)], sems)
    n_targets = out_ref.shape[0]
    for t in range(tiles.shape[0]):
        tiles[t] = rows[:, t * LANES : (t + 1) * LANES].astype(F32)
    slot = lax.broadcasted_iota(jnp.int32, (8, LANES), 1) // 8

    def one(target, carry):
        block = jnp.zeros((8, LANES), F32)
        for q in range(width // 8):
            place = places[q * n_targets + target]
            tile = tiles[lax.shift_right_logical(place, 4)]
            turned = pltpu.roll(tile, ((q + 16 - (place & 15)) & 15) * 8, 1)
            block = jnp.where(slot == q, turned, block)
        out_ref[target] = block
        return carry

    lax.fori_loop(0, n_targets, one, 0, unroll=8)


def make_edges(
    values_hbm, stiff_hbm, lists_hbm, values_ref, stiff_ref, inner_ref, outer_ref, left_ref, right_ref,
    lists_ref, up_ref, down_ref, sems,
):
    fetch([(values_hbm, values_ref), (stiff_hbm, stiff_ref), (lists_hbm, lists_ref)], sems)
    lists = lists_ref[...]
    stiff = stiff_ref[...]
    turned = stiff.T
    component, i, j = lists >> 8, (lists >> 4) & 15, lists & 15
    codes = (
        component * 32 + i * 16 + j,
        component * 32 + (i - 14) * 16 + j,
        component * 128 + i * 8 + j,
        component * 128 + i * 8 + j - 8,
    )
    for side, ref in enumerate((up_ref, down_ref, left_ref, right_ref)):
        first = 0 if side in (0, 2) else CELLS - 2
        for c in range(COMPONENTS):
            for layer in range(2):
                if side < 2:
                    rows = pl.ds(c * 256 + (first + layer) * CELLS, CELLS)
                else:
                    rows = pl.ds(c * 256 + first + layer, CELLS, stride=CELLS)
                ref[pl.ds((c * 2 + layer) * CELLS, CELLS), :] = values_ref[rows, :]
        for layer in range(2):
            source = turned if side < 2 else stiff
            one = source[:, first + layer : first + layer + 1]
            ref[pl.ds(STRIP + layer * CELLS, CELLS), :] = jnp.broadcast_to(one, (CELLS, LANES))
        code = (codes[side][side : side + 1] + 1).astype(F32)
        code = jnp.concatenate([code, jnp.zeros((1, LANES - MARGIN), F32)], axis=1)
        ref[pl.ds(STRIP + 2 * CELLS, 8), :] = jnp.broadcast_to(code, (8, LANES))
    inner_ref[...], outer_ref[...] = by_chip(up_ref[...], down_ref[...])


def restrict(strips, beside, across_ref, along_ref, basis_ref, sub_ref):
    sub_ref[OWN : OWN + 2 * MARGIN] = matmul(across_ref[...], strips.astype(BF16), (0, 0)).astype(BF16)
    sub_ref[OWN + 2 * MARGIN :] = matmul(along_ref[...], beside.astype(BF16), (0, 0)).astype(BF16)
    return matmul(basis_ref[...], sub_ref[...]).astype(BF16).astype(F32)


def start_pass(
    values_ref, stiff_ref, basis_ref, ordered_ref, inner_ref, outer_ref, left_ref, right_ref,
    field_ref, diagonal_ref, across_ref, along_ref, sub_ref, both_ref, up_ref, down_ref,
):
    up_ref[...], down_ref[...] = by_side(inner_ref[...], outer_ref[...])
    turned = stiff_ref[...].T
    field_ref[...] = jnp.zeros_like(field_ref)
    diagonal_ref[...] = jnp.full(diagonal_ref.shape, 4.0, F32)
    for c in range(COMPONENTS):
        for i in range(CELLS):
            rows = values_ref[c * 256 + i * CELLS : c * 256 + (i + 1) * CELLS]
            field_ref[pl.ds(at(c, i), CELLS), :] = rows
            sub_ref[c * 256 + i * CELLS : c * 256 + (i + 1) * CELLS] = rows.astype(BF16)
        for layer in range(2):
            rows = pl.ds((c * 2 + layer) * CELLS, CELLS)
            field_ref[pl.ds(at(c, layer - 2), CELLS), :] = up_ref[rows, :]
            field_ref[pl.ds(at(c, layer + CELLS), CELLS), :] = down_ref[rows, :]
            field_ref[column_of(c, layer - 2), :] = left_ref[rows, :]
            field_ref[column_of(c, layer + CELLS), :] = right_ref[rows, :]
    for i in range(CELLS):
        diagonal_ref[pl.ds(at(0, i), CELLS), :] += jnp.broadcast_to(turned[:, i : i + 1], (CELLS, LANES))
    for layer in range(2):
        rows = pl.ds(STRIP + layer * CELLS, CELLS)
        diagonal_ref[pl.ds(at(0, layer - 2), CELLS), :] += up_ref[rows, :]
        diagonal_ref[pl.ds(at(0, layer + CELLS), CELLS), :] += down_ref[rows, :]
        diagonal_ref[column_of(0, layer - 2), :] += left_ref[rows, :]
        diagonal_ref[column_of(0, layer + CELLS), :] += right_ref[rows, :]

    def chosen(ref, rows):
        code = ref[STRIP + 2 * CELLS : STRIP + 2 * CELLS + 1, 0:MARGIN]
        spot = lax.broadcasted_iota(jnp.int32, (rows, MARGIN), 0).astype(F32) + 1.0
        return jnp.where(spot == code, 1.0, 0.0)

    none = jnp.zeros((STRIP, MARGIN), F32)
    across_ref[...] = jnp.concatenate(
        [
            jnp.concatenate([chosen(up_ref, STRIP), none], axis=1),
            jnp.concatenate([none, chosen(down_ref, STRIP)], axis=1),
        ],
        axis=0,
    ).astype(BF16)
    along_ref[...] = jnp.concatenate(
        [chosen(left_ref, BESIDE), chosen(right_ref, BESIDE)], axis=1
    ).astype(BF16)
    strips = jnp.concatenate([up_ref[0:STRIP], down_ref[0:STRIP]], axis=0)
    beside = jnp.concatenate(
        [field_ref[pl.ds(at(c, i, CELLS), 8), :] for c in range(COMPONENTS) for i in range(CELLS)], axis=0
    )
    coarse = restrict(strips, beside, across_ref, along_ref, basis_ref, sub_ref)
    for target in range(both_ref.shape[0]):
        both_ref[target] = jnp.concatenate([ordered_ref[target], coarse], axis=0).astype(BF16)


def cross_first(both_ref, rows_ref, parts_ref):
    n, k = both_ref.shape[0], both_ref.shape[1] // 2
    both = both_ref[...].astype(F32)
    rows_ref[...] = both[:, :k].reshape(n * k, LANES).astype(BF16)
    parts = matmul(rows_ref[...], both[:, k:].reshape(n * k, LANES).astype(BF16), (0, 0))
    parts_ref[...] = parts[: parts_ref.shape[0] * k].reshape(parts_ref.shape)


def cross_second(rows_ref, column_ref, parts_ref):
    n, k = column_ref.shape[:2]
    parts = matmul(rows_ref[...], column_ref[...].reshape(n * k, LANES).astype(BF16), (0, 0))
    parts_ref[...] = parts[: parts_ref.shape[0] * k].reshape(parts_ref.shape)


def apply_inverse(inverse_hbm, sub_ref, patch_ref, inverse, sems):
    count = sems.shape[0]
    size = inverse.shape[0] // count
    parts = [pl.ds(i * size, size) for i in range(count)]
    chunks = [pltpu.make_async_copy(inverse_hbm.at[p], inverse.at[p], sems.at[i]) for i, p in enumerate(parts)]
    for chunk in chunks:
        chunk.start()
    for chunk, p in zip(chunks, parts):
        chunk.wait()
        patch_ref[p, :] = matmul(inverse[p, :], sub_ref[...])


def spread(depth, local_ref, basis_ref, parts_ref, across_ref, along_ref, field_ref, inner_ref, outer_ref, patch):
    coarse = jnp.sum(parts_ref[...], axis=0).astype(BF16)
    patch[...] = local_ref[...] + matmul(basis_ref[...], coarse, (0, 0))
    field_ref[...] = jnp.zeros_like(field_ref)
    across = matmul(across_ref[...], patch[OWN : OWN + 2 * MARGIN].astype(BF16))
    along = matmul(along_ref[...], patch[OWN + 2 * MARGIN :].astype(BF16))
    for c in range(COMPONENTS):
        for i in range(CELLS):
            n = c * CELLS + i
            field_ref[pl.ds(at(c, i), CELLS), :] = patch[n * CELLS : (n + 1) * CELLS]
            field_ref[pl.ds(at(c, i, CELLS), 8), :] = along[n * 8 : (n + 1) * 8]
        for layer in range(2):
            n = (c * 2 + layer) * CELLS
            field_ref[pl.ds(at(c, layer - 2), CELLS), :] = across[n : n + CELLS]
            field_ref[pl.ds(at(c, layer + CELLS), CELLS), :] = across[STRIP + n : STRIP + n + CELLS]
        part = part_of(depth)
        inner, outer = by_chip(field_ref[pl.ds(at(c, -2), part), :], field_ref[pl.ds(at(c, CELLS - depth), part), :])
        inner_ref[c * part : (c + 1) * part] = inner.astype(BF16)
        outer_ref[c * part : (c + 1) * part] = outer.astype(BF16)


def add_across(depth, field_ref, outer_ref, inner_ref, out_ref, left_ref, right_ref, strip):
    part, layers = part_of(depth), depth + 2
    out_ref[...] = field_ref[...]
    for c in range(COMPONENTS):
        rows = slice(c * part, (c + 1) * part)
        up, down = by_side(inner_ref[rows].astype(F32), outer_ref[rows].astype(F32))
        for first, came in ((-depth, up), (CELLS - 2, down)):
            out_ref[pl.ds(at(c, first), layers * SIDE), :] += came[: layers * SIDE]
    for first, ref in ((-2, left_ref), (CELLS - depth, right_ref)):
        for c in range(COMPONENTS):
            for q in range(layers):
                strip[pl.ds(q * SIDE, SIDE), :] = out_ref[column_of(c, first + q, -ABOVE, SIDE), :]
            strip[layers * SIDE :] = jnp.zeros((part - layers * SIDE, LANES), F32)
            ref[c * part : (c + 1) * part] = strip[...].astype(BF16)


def add_along(depth, field_ref, left_ref, right_ref):
    part = part_of(depth)
    for c in range(COMPONENTS):
        for first, ref in ((-depth, left_ref), (CELLS - 2, right_ref)):
            came = ref[c * part : (c + 1) * part].astype(F32)
            for q in range(depth + 2):
                where = column_of(c, first + q, -ABOVE, SIDE)
                field_ref[where, :] = field_ref[where, :] + came[q * SIDE : (q + 1) * SIDE]


def operate_row(field, diagonal_ref, c, i):
    here = field(c, i)
    beside = field(c, i - 1) + field(c, i + 1) + pltpu.roll(here, 1, 0) + pltpu.roll(here, SIDE - 1, 0)
    return diagonal_ref[pl.ds(at(0, i), SIDE), :] * here - beside


def middle_pass(
    field_ref, left_ref, right_ref, values_ref, diagonal_ref, across_ref, along_ref, basis_ref,
    first_ref, sub_ref, coarse_ref, strips, beside,
):
    first_ref[...] = field_ref[...]
    add_along(3, first_ref, left_ref, right_ref)

    def field(c, i):
        return first_ref[pl.ds(at(c, i), SIDE), :]

    for c in range(COMPONENTS):
        for i in range(-2, CELLS + 2):
            middle = values_ref[pl.ds(at(c, i), SIDE), :] - operate_row(field, diagonal_ref, c, i)
            if 0 <= i < CELLS:
                n = c * CELLS + i
                sub_ref[n * CELLS : (n + 1) * CELLS] = middle[:CELLS].astype(BF16)
                beside[pl.ds(n * 8, 8), :] = middle[CELLS:]
            else:
                n = (c * 2 + (i + 2 if i < 0 else i - CELLS)) * CELLS + (0 if i < 0 else STRIP)
                strips[pl.ds(n, CELLS), :] = middle[:CELLS]
    coarse = restrict(strips[...], beside[...], across_ref, along_ref, basis_ref, sub_ref)
    for target in range(coarse_ref.shape[0]):
        coarse_ref[target] = coarse


def last_pass(field_ref, left_ref, right_ref, first_ref, values_ref, diagonal_ref, solution_ref, final_ref, total):
    total[...] = field_ref[...]
    add_along(1, total, left_ref, right_ref)
    total[...] += first_ref[...]

    def field(c, i):
        return total[pl.ds(at(c, i), SIDE), :]

    for c in range(COMPONENTS):
        for i in range(CELLS):
            rows = slice((c * CELLS + i) * CELLS, (c * CELLS + i + 1) * CELLS)
            solution_ref[rows] = total[pl.ds(at(c, i), CELLS), :]
            applied = operate_row(field, diagonal_ref, c, i)[:CELLS]
            final_ref[rows] = values_ref[pl.ds(at(c, i), CELLS), :] - applied


def trade(lower, upper, axis):
    count = lax.axis_size(axis)
    forward = [(i, i + 1) for i in range(count - 1)]
    backward = [(target, source) for source, target in forward]
    return lax.ppermute(upper, axis, forward), lax.ppermute(lower, axis, backward)


def trade_by_chip(inner, outer):
    count = lax.axis_size(GX)

    def swap(message, start):
        pairs = [(i, i + 1) for i in range(start, count - 1, 2)]
        return lax.ppermute(message, GX, pairs + [(target, source) for source, target in pairs])

    outer = swap(outer, 1)
    return swap(inner, 0), outer


GX, GY = ("z", "core"), "gy"
FIRST, SECOND = ("core", "gy"), "z"


def per_device(residual, stiffness, local_inverse, coarse_basis, coarse_rows, send_rows, partition_map):
    inverse, basis, lists = local_inverse[0, 0], coarse_basis[0, 0], send_rows[0, 0]
    k, order = coarse_rows.shape[2:]
    n_first, n_second = lax.axis_size(FIRST), lax.axis_size(SECOND)
    values = residual.reshape(OWN, LANES)
    swap = functools.partial(lax.all_to_all, split_axis=0, concat_axis=0, tiled=True)

    own, field, edge = ((OWN, LANES), F32), ((FIELD, LANES), F32), ((EDGE, LANES), F32)
    sub_kind, patch = ((OWN + 4 * MARGIN, LANES), BF16), ((OWN + 4 * MARGIN, LANES), F32)
    copies, sums = ((n_first, k, LANES), F32), ((n_second, k, LANES), F32)
    values, stiffness, inner, outer, left, right = call(
        make_edges, [own, (stiffness.shape, F32), *[edge] * 4], values, stiffness, lists, fetched=3,
        scratch=[(lists.shape, jnp.int32), edge, edge],
    )
    ordered, basis = call(
        functools.partial(order_rows, n_second * k), [copies, (basis.shape, BF16)],
        coarse_rows[0, 0], partition_map, basis, inner, fetched=3,
        scratch=[((k, order), BF16), pltpu.SMEM(partition_map.shape, jnp.int32), ((order // LANES, k, LANES), F32)],
    )
    inner, outer = trade_by_chip(inner, outer)
    left, right = trade(left, right, GY)
    ambient, diagonal, across, along, sub, both = call(
        start_pass,
        [
            field, ((PLANE, LANES), F32), ((2 * STRIP, 2 * MARGIN), BF16), ((BESIDE, 2 * MARGIN), BF16), sub_kind,
            ((n_first, 2 * k, LANES), BF16),
        ],
        values, stiffness, basis, ordered, inner, outer, left, right, scratch=[edge, edge],
    )

    def correct(depth, sub, parts):
        part = ((COMPONENTS * part_of(depth), LANES), BF16)
        [local] = call(
            apply_inverse, [patch], inverse, sub, fetched=1, copies=4, scratch=[(inverse.shape, BF16)],
            cost=(inverse.size * LANES * 2, inverse.size * 2),
        )
        y, inner, outer = call(
            functools.partial(spread, depth), [field, part, part],
            local, basis, swap(parts, SECOND), across, along, scratch=[patch],
        )
        y, to_left, to_right = call(
            functools.partial(add_across, depth), [field, part, part], y, *trade_by_chip(inner, outer)[::-1],
            scratch=[((part_of(depth), LANES), F32)],
        )
        return (y, *trade(to_left, to_right, GY))

    crossing, parts = call(cross_first, [((n_first * k, LANES), BF16), sums], swap(both, FIRST))
    first, sub, coarse = call(
        middle_pass, [field, sub_kind, copies], *correct(3, sub, parts), ambient, diagonal, across, along, basis,
        scratch=[((2 * STRIP, LANES), F32), ((BESIDE, LANES), F32)],
    )
    [parts] = call(cross_second, [sums], crossing, swap(coarse, FIRST))
    total, final = call(
        last_pass, [own, own], *correct(1, sub, parts), first, ambient, diagonal, scratch=[field]
    )
    return total.reshape(residual.shape), final.reshape(residual.shape)


def solution(mesh):
    split = Mesh(mesh.devices.reshape(-1, 2, mesh.devices.shape[1]), ("z", "core", "gy"))
    cells = P(None, GX, GY, None)
    placed = (cells, P(GX, GY), *[P(GX, GY, None, None)] * 4, P())
    return jax.shard_map(per_device, mesh=split, in_specs=placed, out_specs=(cells, cells), check_vma=False)
```
